32 devices in a mesh: leaf: 32 (over z, y, x, core).
Axes of the slice: x: 2, y: 2, z: 4, core: 2. Of those that a mesh axis runs over, the one named last changes fastest.
Arguments:
- leaf_bases: float32 [1024, 64, 128], P('leaf'), may hold values from -0.6 to 0.6
- transfers: float32 [512, 64, 128], P('leaf'), may hold values from -0.5 to 0.5
- leaf_blocks: float32 [64, 64, 8192], P(None, None, 'leaf'), may hold values from -6 to 6
- parent_blocks: float32 [64, 64, 8192], P(None, None, 'leaf'), may hold values from -6 to 6
- leaf_rows: int32 [8192], P('leaf'), may hold values from 0 to 31
- leaf_slots: int32 [8192], P('leaf'), may hold values from 0 to 127, as said below
- leaf_requests: int32 [32, 128], P('leaf'), may hold values from 0 to 31
- parent_rows: int32 [8192], P('leaf'), may hold values from 0 to 15
- parent_slots: int32 [8192], P('leaf'), may hold values from 0 to 127, as said below
- parent_requests: int32 [32, 128], P('leaf'), may hold values from 0 to 15
- block_counts: int32 [32, 2], P('leaf'), may hold values from 160 to 256, as said below
Outputs:
- leaf_basis: float32 [1024, 64, 128], P('leaf')
- new_transfers: float32 [512, 64, 128], P('leaf')
- leaf_coupling: float32 [64, 64, 8192], P(None, None, 'leaf')
- parent_coupling: float32 [64, 64, 8192], P(None, None, 'leaf')
The draws below stay inside these ranges and needn't reach their ends.
Inputs may be any that keep to these rules, and one draw needn't show every extreme that they name: `leaf_slots`: slot s names a cluster of device s // 4; several blocks of a device may name one slot, and every slot is named by some block of each device. `parent_slots`: slot s names a cluster of device s // 4; several blocks of a device may name one slot, and every slot is named by some block of each device. `block_counts`: column 0 lies in 160 to 256, column 1 in 160 to 256; live blocks are the first ones of a device.
All inputs are finite; a program needn't handle non-finite values.
Results may differ from the reference program's by a relative error of at most 0.0003.
Values sent between devices are 32-bit elements; how exact they have to be, the bound alone decides.
No kernel may reach another device: no remote copies, remote signals or barrier semaphores. Data moves between devices by JAX's collectives and lax.ppermute only.
A program may use at most 192 MiB of HBM per device.

```python
import jax
import jax.numpy as jnp
from jax import lax

K = 64
P_SIZE = 128
LEAF_DEV = 32
BLK_DEV = 256
PBLK_DEV = 256
PAR_DEV = 16
LEAVES = 1024
PARENTS = 512
CAP = 4
PCAP = 4
SLOTS = 128
PSLOTS = 128
LEAF_BLOCKS = 8192
PAR_BLOCKS = 8192
N_LEAF = 32


def slot_plan(key, per_dev, capacity):
    slot_total = N_LEAF * capacity
    extra_count = per_dev - slot_total
    hot_device = jax.random.randint(jax.random.fold_in(key, 7), (), 0, N_LEAF)
    base_keys = jax.random.split(jax.random.fold_in(key, 11), N_LEAF)
    order_keys = jax.random.split(jax.random.fold_in(key, 13), N_LEAF)

    def one_base(device_key):
        return jax.random.permutation(device_key, slot_total).astype(jnp.int32)
    base = jax.vmap(one_base)(base_keys)
    extra_any = jax.random.randint(jax.random.fold_in(key, 17), (N_LEAF, extra_count), 0, slot_total)
    extra_hot = hot_device * capacity + jax.random.randint(jax.random.fold_in(key, 19), (N_LEAF, extra_count), 0, capacity)
    pick_hot = jax.random.randint(jax.random.fold_in(key, 23), (N_LEAF, extra_count), 0, 2)
    extra = jnp.where(pick_hot == 1, extra_hot, extra_any).astype(jnp.int32)
    joined = jnp.concatenate([base, extra], axis=1)

    def one_order(device_key, row_values):
        return jnp.take(row_values, jax.random.permutation(device_key, per_dev), axis=0)
    mixed = jax.vmap(one_order)(order_keys, joined)
    return mixed.reshape(-1).astype(jnp.int32)


def draw_leaf_slots(key, part):
    return slot_plan(jax.random.fold_in(key, 1), BLK_DEV, CAP)


def draw_parent_slots(key, part):
    return slot_plan(jax.random.fold_in(key, 2), PBLK_DEV, PCAP)


def draw_block_counts(key, part):
    keys = jax.random.split(jax.random.fold_in(key, 3), 3)
    leaf_part = jax.random.randint(keys[0], (N_LEAF,), 5 * BLK_DEV // 8, BLK_DEV + 1)
    parent_part = jax.random.randint(keys[1], (N_LEAF,), 5 * PBLK_DEV // 8, PBLK_DEV + 1)
    picked = jax.random.permutation(keys[2], N_LEAF)
    leaf_part = leaf_part.at[picked[0]].set(BLK_DEV).at[picked[1]].set(5 * BLK_DEV // 8)
    parent_part = parent_part.at[picked[2]].set(PBLK_DEV).at[picked[3]].set(5 * PBLK_DEV // 8)
    return jnp.stack([leaf_part, parent_part], axis=1).astype(jnp.int32)


def place_ends(values, stream_key, least, largest):
    longest = values.shape.index(max(values.shape))
    spots = []
    for shift in (0, 1):
        where = [jax.random.randint(jax.random.fold_in(stream_key, axis), (), 0, length) for axis, length in enumerate(values.shape)]
        where[longest] = (where[longest] + shift) % values.shape[longest]
        spots.append(tuple(where))
    return values.at[spots[0]].set(least).at[spots[1]].set(largest)


def levels(own_key, shape, pieces, low, largest):
    loudness = 1.0
    for position, shards_of in pieces:
        draws = jax.random.uniform(jax.random.fold_in(jax.random.fold_in(own_key, 6), position), (shards_of,), jnp.float32, low / len(pieces), largest / len(pieces))
        loudness = loudness * jnp.repeat(jnp.exp(draws), shape[position] // shards_of).reshape((-1,) + (1,) * (len(shape) - 1 - position))
    return loudness


def normal_values(own_key, extent, width, limit, shards=(), held_as=jnp.bfloat16):
    entries = width * jax.random.normal(own_key, extent, jnp.float32)
    if shards:
        entries = entries * levels(own_key, extent, shards, -0.22, 0.18)
    return jnp.clip(entries, -limit, limit).astype(held_as)


def setup_inputs(seed: int = 0) -> dict:
    key_of = jax.random.split(jax.random.key(seed), 12)
    return {
        "leaf_bases": normal_values(key_of[0], (LEAVES, K, P_SIZE), 0.09, 0.6, ((0, 32),), jnp.float32),
        "transfers": normal_values(key_of[1], (PARENTS, K, 2 * K), (2 * K) ** -0.5, 0.5, ((0, 32),), jnp.float32),
        "leaf_blocks": normal_values(key_of[2], (K, K, LEAF_BLOCKS), 1.0, 6.0, ((2, 32),), jnp.float32),
        "parent_blocks": normal_values(key_of[3], (K, K, PAR_BLOCKS), 1.0, 6.0, ((2, 32),), jnp.float32),
        "leaf_rows": place_ends(jax.random.randint(key_of[4], (LEAF_BLOCKS,), 0, LEAF_DEV), jax.random.fold_in(key_of[4], 1), 0, LEAF_DEV - 1).astype(jnp.int32),
        "leaf_slots": draw_leaf_slots(jax.random.fold_in(key_of[11], 71), 0),
        "leaf_requests": place_ends(jax.random.randint(key_of[6], (N_LEAF, SLOTS), 0, LEAF_DEV), jax.random.fold_in(key_of[6], 1), 0, LEAF_DEV - 1).astype(jnp.int32),
        "parent_rows": place_ends(jax.random.randint(key_of[7], (PAR_BLOCKS,), 0, PAR_DEV), jax.random.fold_in(key_of[7], 1), 0, PAR_DEV - 1).astype(jnp.int32),
        "parent_slots": draw_parent_slots(jax.random.fold_in(key_of[11], 71), 0),
        "parent_requests": place_ends(jax.random.randint(key_of[9], (N_LEAF, PSLOTS), 0, PAR_DEV), jax.random.fold_in(key_of[9], 1), 0, PAR_DEV - 1).astype(jnp.int32),
        "block_counts": draw_block_counts(jax.random.fold_in(key_of[11], 71), 0),
    }


PRECISE = lax.Precision.HIGHEST

def leaf_factors(leaf_bases):
    leaf_gram = jnp.einsum('lkp,ljp->lkj', leaf_bases, leaf_bases, precision=PRECISE)
    leaf_lower = jnp.linalg.cholesky(leaf_gram)
    leaf_basis = jax.scipy.linalg.solve_triangular(leaf_lower, leaf_bases, lower=True)
    return (leaf_lower, leaf_basis)

def parent_merge(leaf_lower, transfers):
    parent_total = transfers.shape[0]
    rank_dim = transfers.shape[1]
    child_upper = jnp.swapaxes(leaf_lower, 1, 2).reshape(parent_total, 2, rank_dim, rank_dim)
    child_pieces = transfers.reshape(parent_total, rank_dim, 2, rank_dim)
    stacked = jnp.einsum('pcik,pkcj->pcij', child_upper, child_pieces, precision=PRECISE)
    parent_gram = jnp.einsum('pcki,pckj->pij', stacked, stacked, precision=PRECISE)
    parent_lower = jnp.linalg.cholesky(parent_gram)
    wide_lower = jnp.broadcast_to(parent_lower[:, None], (parent_total, 2, rank_dim, rank_dim))
    solved = jax.scipy.linalg.solve_triangular(wide_lower, jnp.swapaxes(stacked, 2, 3), lower=True)
    new_transfers = jnp.transpose(solved, (0, 3, 1, 2)).reshape(parent_total, rank_dim, 2 * rank_dim)
    return (new_transfers, parent_lower)

def couple_level(upper_table, blocks, rows, slots, requests, counts, per_dev, clusters_dev):
    capacity = requests.shape[1] // N_LEAF
    rank_dim = blocks.shape[0]

    def one_owner(owner_id):
        start = owner_id * per_dev
        block_slice = lax.dynamic_slice_in_dim(blocks, start, per_dev, 2)
        row_ids = lax.dynamic_slice_in_dim(rows, start, per_dev, 0)
        slot_ids = lax.dynamic_slice_in_dim(slots, start, per_dev, 0)
        wanted = lax.dynamic_index_in_dim(requests, owner_id, 0, keepdims=False)
        column_local = jnp.take(wanted, slot_ids, axis=0)
        row_global = owner_id * clusters_dev + row_ids
        column_global = slot_ids // capacity * clusters_dev + column_local
        row_factors = jnp.take(upper_table, row_global, axis=2)
        column_factors = jnp.take(upper_table, column_global, axis=2)
        left_products = jnp.einsum('ikb,kjb->ijb', row_factors, block_slice, precision=PRECISE)
        coupled = jnp.einsum('ijb,ljb->ilb', left_products, column_factors, precision=PRECISE)
        live_mask = jnp.arange(per_dev, dtype=jnp.int32) < counts[owner_id]
        return jnp.where(live_mask[None, None, :], coupled, jnp.zeros_like(coupled))
    per_owner = lax.map(one_owner, jnp.arange(N_LEAF, dtype=jnp.int32))
    return jnp.transpose(per_owner, (1, 2, 0, 3)).reshape(rank_dim, rank_dim, -1)

def reference(leaf_bases, transfers, leaf_blocks, parent_blocks, leaf_rows, leaf_slots, leaf_requests, parent_rows, parent_slots, parent_requests, block_counts):
    leaf_lower, leaf_basis = leaf_factors(leaf_bases)
    new_transfers, parent_lower = parent_merge(leaf_lower, transfers)
    leaf_table = jnp.transpose(leaf_lower, (2, 1, 0))
    parent_table = jnp.transpose(parent_lower, (2, 1, 0))
    leaf_coupling = couple_level(leaf_table, leaf_blocks, leaf_rows, leaf_slots, leaf_requests, block_counts[:, 0], BLK_DEV, LEAF_DEV)
    parent_coupling = couple_level(parent_table, parent_blocks, parent_rows, parent_slots, parent_requests, block_counts[:, 1], PBLK_DEV, PAR_DEV)
    return (leaf_basis, new_transfers, leaf_coupling, parent_coupling)
```

```python
import functools

import jax
import jax.numpy as jnp
from jax import lax
from jax.experimental import pallas as pl
from jax.experimental.pallas import tpu as pltpu
from jax.sharding import PartitionSpec as P

F32=jnp.float32; BF16=jnp.bfloat16
HI=lax.Precision.HIGHEST
NT=(((1,),(1,)),((),()))
NN=(((1,),(0,)),((),()))

def seg_tiles(k, tiles):
    p, s = divmod(k, 8)
    low = [(8*(tiles-p)+s, jv) for jv in range(tiles-p, tiles)] if p else []
    return low + [(k, jv) for jv in range(p, tiles)]

def chunk_tiles(e):
    if e < 16:
        return seg_tiles(e, 8) + seg_tiles(e+16, 8)
    return [(32 + 4*(e-16) + s, jv) for s in (1, 0, 3, 2) for jv in range(4, 8)]

def split(x):
    hi = x.astype(BF16)
    return hi, (x - hi.astype(F32)).astype(BF16)

def factor_kernel(u_ref, e_ref, table_ref, r_ref, rinv_ref, nat, gd, a_ref):
    L = u_ref.shape[0]; Pn = e_ref.shape[0]; C = L+Pn
    lane = lax.broadcasted_iota(jnp.int32, (64,128), 1)
    left = lane < 64
    left32 = left[:32]
    def gram(l, c):
        u = u_ref[l]
        g = lax.dot_general(u, jnp.concatenate([u,u],0), NT, precision=HI, preferred_element_type=F32)
        gd[l] = g
        nat[pl.ds(l*32,32),:] = jnp.where(left32, g[:32], g[32:])
        return c
    lax.fori_loop(0, L, gram, 0, unroll=4)
    def parent(p, c):
        e = e_ref[p]
        er = pltpu.roll(e, 64, 1)
        e0 = jnp.where(left, e, er); e1 = jnp.where(left, er, e)
        t0 = lax.dot_general(gd[2*p][:, :64], e0, NN, precision=HI, preferred_element_type=F32)
        t1 = lax.dot_general(gd[2*p+1][:, :64], e1, NN, precision=HI, preferred_element_type=F32)
        est = jnp.concatenate([e0,e1],0).T[:64]
        g = lax.dot_general(est, jnp.concatenate([t0,t1],0), NN, precision=HI, preferred_element_type=F32)
        nat[pl.ds((L+p)*32,32),:] = jnp.where(left32, g[:32], g[32:])
        return c
    lax.fori_loop(0, Pn, parent, 0, unroll=4)
    zeros = jnp.zeros((128-C,128), F32)
    for i in range(32):
        x = jnp.concatenate([nat[pl.ds(i, C, 32), :], zeros], 0).T
        a_ref[i] = x[:64]
        a_ref[i+32] = x[64:]
    live = lax.broadcasted_iota(jnp.int32, (1,128), 1) < C
    sub = lax.broadcasted_iota(jnp.int32, (8,128), 0)
    for p in range(8):
        b = 8*p
        T = [a_ref[b+kk, b:b+8, :] for kk in range(8)]
        for kk in range(8):
            inv = lax.rsqrt(jnp.where(live, T[kk][kk:kk+1,:], 1.0))
            row = jnp.where(sub >= kk, T[kk]*inv, 0.0)
            rinv_ref[pl.ds(b+kk,1), :] = inv
            r_ref[b+kk, b:b+8, :] = row
            for k2 in range(kk+1, 8):
                T[k2] = T[k2] - row[k2:k2+1,:]*row
        for q in range(p+1, 8):
            T = []
            for kk in range(8):
                s = a_ref[b+kk, 8*q:8*q+8, :]
                for t in range(kk):
                    s = s - r_ref[b+t, pl.ds(b+kk,1), :]*T[t]
                T.append(s*rinv_ref[pl.ds(b+kk,1), :])
                r_ref[b+kk, 8*q:8*q+8, :] = T[kk]
        for q in range(p+1, 8):
            def upd(h, c):
                i0 = 8*q + 4*h
                acc = [[a_ref[i0+u, 8*j:8*j+8, :] for j in range(q,8)] for u in range(4)]
                for kk in range(8):
                    v = [r_ref[b+kk, 8*j:8*j+8, :] for j in range(q,8)]
                    for u in range(4):
                        m = r_ref[b+kk, pl.ds(i0+u,1), :]
                        for j in range(8-q):
                            acc[u][j] = acc[u][j] - m*v[j]
                for u in range(4):
                    for j in range(q,8):
                        a_ref[i0+u, 8*j:8*j+8, :] = acc[u][j-q]
                return c
            lax.fori_loop(0, 2, upd, 0, unroll=True)
    row = lax.broadcasted_iota(jnp.int32, (C,128), 0)
    col = lax.broadcasted_iota(jnp.int32, (C,128), 1)
    eye = (row == col).astype(F32).astype(BF16)
    eye2 = jnp.concatenate([eye, eye], 1)
    for e in range(18):
        ch = jnp.concatenate([r_ref[k, 8*j:8*j+8, :] for k, j in chunk_tiles(e)], 0)
        hi, lo = split(ch)
        table_ref[e] = lax.dot_general(eye2, jnp.concatenate([hi,lo],1), NT, preferred_element_type=F32)

def factor(u, e):
    L, Pn = u.shape[0], e.shape[0]; C = L+Pn
    return pl.pallas_call(factor_kernel,
        out_shape=(jax.ShapeDtypeStruct((18,C,128),F32), jax.ShapeDtypeStruct((64,64,128),F32), jax.ShapeDtypeStruct((64,128),F32)),
        scratch_shapes=[pltpu.VMEM((C*32,128),F32), pltpu.VMEM((L,64,128),F32), pltpu.VMEM((64,64,128),F32)],
        compiler_params=pltpu.CompilerParams(vmem_limit_bytes=40*2**20),
        name="factor")(u, e)

def unpack(v):
    lane = lax.broadcasted_iota(jnp.int32, (8,128), 1)
    sub = lax.broadcasted_iota(jnp.int32, (8,128), 0)
    half = lane & 63
    left = lane < 64
    v0, v1 = v[0:8], v[8:16]
    w0, w1 = pltpu.roll(v0, 64, 1), pltpu.roll(v1, 64, 1)
    y = jnp.where(sub < 4, v[16:17], v[17:18])
    z = pltpu.roll(pltpu.roll(y, 0, 1, stride=16, stride_axis=0), 0, 1, stride=16, stride_axis=0)
    parts = [
        jnp.where(left, v0, w0),
        jnp.where(left, v1, w1),
        jnp.where(left, w0, v0),
        jnp.where(left, w1, v1),
        jnp.where(left, z, pltpu.roll(z, 64, 1)),
        jnp.where(left, pltpu.roll(v1, 104, 1), pltpu.roll(v1, 40, 1)),
        jnp.where(left, pltpu.roll(v0, 112, 1), pltpu.roll(v0, 48, 1)),
        jnp.where(left, pltpu.roll(v1, 56, 1), pltpu.roll(v1, 120, 1)),
    ]
    return jnp.concatenate([x if p == 0 else jnp.where(half >= 8*p, x, 0.0) for p, x in enumerate(parts)], 0)

def mix(x):
    left = lax.broadcasted_iota(jnp.int32, x.shape, 1) < 64
    hi = x.astype(BF16).astype(F32)
    return jnp.where(left, hi, x - hi).astype(BF16)

def left_kernel(base, clusters, total, rows_ref, table_ref, s_ref, out_ref, m_ref, lhs_ref):
    h = pl.program_id(0)
    @pl.when(h == 0)
    def _():
        def prep(c, _):
            lhs_ref[c] = mix(unpack(table_ref[pl.ds(base + c, 18, total), :]))
            return _
        lax.fori_loop(0, clusters, prep, 0, unroll=4)
    for k in range(32):
        m_ref[pl.ds(k, 128, 32), :] = jnp.concatenate([s_ref[k], s_ref[k+32]], 0).T
    left = lax.broadcasted_iota(jnp.int32, (32,128), 1) < 64
    def one(b, _):
        m = m_ref[pl.ds(pl.multiple_of(b*32, 32), 32), :]
        t = pltpu.roll(m, 64, 1)
        hi, lo = split(jnp.concatenate([jnp.where(left, m, t), jnp.where(left, t, m)], 0))
        a = lhs_ref[rows_ref[h*128 + b]]
        res = lax.dot_general(jnp.concatenate([a, a], 1), jnp.concatenate([hi,hi,lo,lo], 0), NN, preferred_element_type=F32)
        out_ref[b] = mix(res)
        return _
    lax.fori_loop(0, 128, one, 0, unroll=8)

def left_products(rows, table, blocks, base, clusters):
    total = table.shape[0]//18
    B = blocks.shape[2]
    return pl.pallas_call(functools.partial(left_kernel, base, clusters, total),
        grid=(B//128,),
        in_specs=[pl.BlockSpec(memory_space=pltpu.SMEM), pl.BlockSpec(table.shape, lambda h: (0,0)),
                  pl.BlockSpec((64,64,128), lambda h: (0,0,h))],
        out_specs=pl.BlockSpec((128,64,128), lambda h: (h,0,0)),
        out_shape=jax.ShapeDtypeStruct((B,64,128), BF16),
        scratch_shapes=[pltpu.VMEM((128*32,128),F32), pltpu.VMEM((clusters,64,128),BF16)],
        compiler_params=pltpu.CompilerParams(vmem_limit_bytes=40*2**20), name="left")(rows, table, blocks)

def close_kernel(cap, offset, wide, slots_ref, count_ref, p_ref, f_ref, out_ref, c_ref, w_ref):
    h = pl.program_id(0)
    peers = f_ref.shape[0]//(18*wide)
    @pl.when(h == 0)
    def _():
        def prep(n, _):
            for t in range(cap):
                hi, lo = split(unpack(f_ref[pl.ds(n*18*wide + offset + t, 18, wide), :]))
                w_ref[n*cap + t] = jnp.concatenate([hi, lo], 1)
            return _
        lax.fori_loop(0, peers, prep, 0, unroll=max(1, 4//cap))
    def one(b, _):
        a = p_ref[b]
        res = lax.dot_general(jnp.concatenate([a, a], 1), w_ref[slots_ref[h*128 + b]], NT, preferred_element_type=F32)
        c_ref[pl.ds(pl.multiple_of(b*32, 32), 32), :] = jnp.concatenate([res[:32], res[32:]], 1)
        return _
    lax.fori_loop(0, 128, one, 0, unroll=8)
    live = lax.broadcasted_iota(jnp.int32, (64,128), 1) + h*128 < count_ref[0]
    for i in range(32):
        x = c_ref[pl.ds(i, 128, 32), :].T
        out_ref[i] = jnp.where(live, x[:64], 0.0)
        out_ref[i+32] = jnp.where(live, x[64:], 0.0)

def close(slots, count, prods, fetched, cap, offset, wide):
    B = prods.shape[0]
    S = fetched.shape[0]//(18*wide)*cap
    return pl.pallas_call(functools.partial(close_kernel, cap, offset, wide),
        grid=(B//128,),
        in_specs=[pl.BlockSpec(memory_space=pltpu.SMEM), pl.BlockSpec(memory_space=pltpu.SMEM),
                  pl.BlockSpec((128,64,128), lambda h: (h,0,0)), pl.BlockSpec(fetched.shape, lambda h: (0,0))],
        out_specs=pl.BlockSpec((64,64,128), lambda h: (0,0,h)),
        out_shape=jax.ShapeDtypeStruct((64,64,B), F32),
        scratch_shapes=[pltpu.VMEM((128*32,128),F32), pltpu.VMEM((S,64,256),BF16)],
        compiler_params=pltpu.CompilerParams(vmem_limit_bytes=48*2**20), name="close")(slots, count, prods, fetched)

def gather_kernel(idx_ref, table_ref, out_ref):
    C = table_ref.shape[1]; S = idx_ref.shape[1]
    pad = jnp.zeros((128-C, 128), F32)
    hot = (lax.broadcasted_iota(jnp.int32, (128,S), 0) == idx_ref[...]).astype(F32).T.astype(BF16)
    hot = jnp.concatenate([hot, hot], 1)
    for e in range(18):
        hi, lo = split(jnp.concatenate([table_ref[e], pad], 0))
        res = lax.dot_general(hot, jnp.concatenate([hi, lo], 0), NN, preferred_element_type=F32)
        if out_ref.ndim == 4:
            out_ref[:, e] = res.reshape(out_ref.shape[0], 8, 128)
        else:
            out_ref[e] = res

def gather(idx, table):
    n, wide = idx.shape
    direct = wide == 8
    shape = (n,18,wide,128) if direct else (18,n*wide,128)
    out = pl.pallas_call(gather_kernel, out_shape=jax.ShapeDtypeStruct(shape,F32),
        compiler_params=pltpu.CompilerParams(vmem_limit_bytes=32*2**20), name="gather")(idx.reshape(1,-1), table)
    return out if direct else out.reshape(18,n,wide,128).transpose(1,0,2,3)

def basis_kernel(u_ref, e_ref, table_ref, r_ref, rinv_ref, basis_ref, nt_ref, x_ref, nat):
    L = u_ref.shape[0]; Pn = e_ref.shape[0]; C = L+Pn
    sub = lax.broadcasted_iota(jnp.int32, (8,128), 0)
    zero = jnp.zeros((8,128), F32)
    for q in range(8):
        def rows(h, _):
            acc = [[zero]*q for u in range(4)]
            for t in range(8*q):
                v = [x_ref[t, 8*j:8*j+8, :] for j in range(t//8+1)]
                for u in range(4):
                    m = r_ref[t, pl.ds(8*q+4*h+u,1), :]
                    for j in range(t//8+1):
                        acc[u][j] = acc[u][j] - m*v[j]
            for u in range(4):
                for j in range(q):
                    x_ref[8*q+4*h+u, 8*j:8*j+8, :] = acc[u][j]
            return _
        if q:
            lax.fori_loop(0, 2, rows, 0, unroll=True)
        for j in range(q+1):
            T = []
            for u in range(8):
                s = (sub == u).astype(F32) if j == q else x_ref[8*q+u, 8*j:8*j+8, :]
                for t in range(u):
                    s = s - r_ref[8*q+t, pl.ds(8*q+u,1), :]*T[t]
                T.append(s*rinv_ref[pl.ds(8*q+u,1), :])
                x_ref[8*q+u, 8*j:8*j+8, :] = T[u]
        for j in range(q+1, 8):
            for u in range(8):
                x_ref[8*q+u, 8*j:8*j+8, :] = zero
    for i in range(32):
        nat[pl.ds(i, C, 32), :] = jnp.concatenate([x_ref[i], x_ref[i+32]], 0).T[:C]
    left32 = lax.broadcasted_iota(jnp.int32, (32,128), 1) < 64
    left = lax.broadcasted_iota(jnp.int32, (64,128), 1) < 64
    def inverse(c):
        m = nat[pl.ds(c*32,32),:]
        t = pltpu.roll(m, 64, 1)
        return jnp.concatenate([jnp.where(left32, m, t), jnp.where(left32, t, m)], 0)[:, :64]
    def leaf(l, _):
        basis_ref[l] = lax.dot_general(inverse(l), u_ref[l], NN, precision=HI, preferred_element_type=F32)
        return _
    lax.fori_loop(0, L, leaf, 0, unroll=4)
    def parent(p, _):
        e = e_ref[p]
        er = pltpu.roll(e, 64, 1)
        est = jnp.concatenate([jnp.where(left, e, er), jnp.where(left, er, e)],0).T[:64]
        w = lax.dot_general(inverse(L+p), est, NN, precision=HI, preferred_element_type=F32)
        wr = pltpu.roll(w, 64, 1)
        r0 = unpack(table_ref[pl.ds(2*p, 18, C), :])[:, :64]
        r1 = unpack(table_ref[pl.ds(2*p+1, 18, C), :])[:, :64]
        n0 = lax.dot_general(r0, jnp.concatenate([w,w],0)[:, :64], NT, precision=HI, preferred_element_type=F32)
        n1 = lax.dot_general(r1, jnp.concatenate([wr,wr],0)[:, :64], NT, precision=HI, preferred_element_type=F32)
        nt_ref[p] = jnp.where(left, n0, n1)
        return _
    lax.fori_loop(0, Pn, parent, 0, unroll=4)

def bases(u, e, table, r, rinv):
    C = u.shape[0]+e.shape[0]
    return pl.pallas_call(basis_kernel,
        out_shape=(jax.ShapeDtypeStruct(u.shape,F32), jax.ShapeDtypeStruct(e.shape,F32)),
        scratch_shapes=[pltpu.VMEM((64,64,128),F32), pltpu.VMEM((C*32,128),F32)],
        compiler_params=pltpu.CompilerParams(vmem_limit_bytes=40*2**20), name="basis")(u, e, table, r, rinv)

def per_device(
    leaf_bases, transfers, leaf_blocks, parent_blocks, leaf_rows, leaf_slots, leaf_requests,
    parent_rows, parent_slots, parent_requests, block_counts,
):
    leaves = leaf_bases.shape[0]
    parents = transfers.shape[0]
    peers = lax.axis_size("leaf")
    cap = leaf_requests.shape[1] // peers
    pcap = parent_requests.shape[1] // peers
    wide = cap + pcap
    wanted = jnp.concatenate(
        [leaf_requests[0].reshape(peers, cap), leaves + parent_requests[0].reshape(peers, pcap)], 1
    )
    wanted_here = lax.all_to_all(wanted, "leaf", 0, 0, tiled=True)
    table, r, rinv = factor(leaf_bases, transfers)
    sent = gather(wanted_here, table)
    fetched = lax.all_to_all(sent, "leaf", 0, 0, tiled=True).reshape(-1, 128)
    flat = table.reshape(-1, 128)
    leaf_left = left_products(leaf_rows, flat, leaf_blocks, 0, leaves)
    parent_left = left_products(parent_rows, flat, parent_blocks, leaves, parents)
    leaf_basis, new_transfers = bases(leaf_bases, transfers, flat, r, rinv)
    leaf_coupling = close(leaf_slots, block_counts[0, :1], leaf_left, fetched, cap, 0, wide)
    parent_coupling = close(parent_slots, block_counts[0, 1:], parent_left, fetched, pcap, cap, wide)
    return (leaf_basis, new_transfers, leaf_coupling, parent_coupling)


def solution(mesh):
    rows = P("leaf", None, None)
    blocks = P(None, None, "leaf")
    ids = P("leaf")
    per_owner = P("leaf", None)
    return jax.shard_map(
        per_device,
        mesh=mesh,
        in_specs=(rows, rows, blocks, blocks, ids, ids, per_owner, ids, ids, per_owner, per_owner),
        out_specs=(rows, rows, blocks, blocks),
        check_vma=False,
    )
```

```python
import functools

import jax
import jax.numpy as jnp
from jax import lax
from jax.experimental import pallas as pl
from jax.experimental.pallas import tpu as pltpu
from jax.sharding import PartitionSpec as P

F32=jnp.float32; BF16=jnp.bfloat16
HI=lax.Precision.HIGHEST
NT=(((1,),(1,)),((),()))
NN=(((1,),(0,)),((),()))

def seg_tiles(k, tiles):
    p, s = divmod(k, 8)
    low = [(8*(tiles-p)+s, jv) for jv in range(tiles-p, tiles)] if p else []
    return low + [(k, jv) for jv in range(p, tiles)]

def chunk_tiles(e):
    if e < 16:
        return seg_tiles(e, 8) + seg_tiles(e+16, 8)
    return [(32 + 4*(e-16) + s, jv) for s in (1, 0, 3, 2) for jv in range(4, 8)]

def params(us, mib):
    return dict(
        cost_estimate=pl.CostEstimate(flops=int(us*1.15e9), bytes_accessed=0, transcendentals=0),
        compiler_params=pltpu.CompilerParams(vmem_limit_bytes=mib*2**20),
    )

def split(x):
    hi = x.astype(BF16)
    return hi, (x - hi.astype(F32)).astype(BF16)

def factor_kernel(u_hbm, e_hbm, table_ref, r_hbm, rinv_ref, nat, gd, a_ref, u_ref, e_ref, r_ref, usem, esem, rsem):
    L = u_ref.shape[0]; Pn = e_ref.shape[0]; C = L+Pn
    part = L//4
    u_in = [pltpu.make_async_copy(u_hbm.at[pl.ds(i*part, part)], u_ref.at[pl.ds(i*part, part)], usem.at[i]) for i in range(4)]
    e_in = pltpu.make_async_copy(e_hbm, e_ref, esem)
    r_out = [pltpu.make_async_copy(r_ref.at[pl.ds(8*p, 8)], r_hbm.at[pl.ds(8*p, 8)], rsem.at[p]) for p in range(8)]
    for copy in u_in + [e_in]:
        copy.start()
    lane = lax.broadcasted_iota(jnp.int32, (64,128), 1)
    left = lane < 64
    left32 = left[:32]
    def gram(l, c):
        u = u_ref[l]
        g = lax.dot_general(u, jnp.concatenate([u,u],0), NT, precision=HI, preferred_element_type=F32)
        gd[l] = g
        nat[pl.ds(l*32,32),:] = jnp.where(left32, g[:32], g[32:])
        return c
    for i in range(4):
        u_in[i].wait()
        lax.fori_loop(i*part, (i+1)*part, gram, 0, unroll=part)
    e_in.wait()
    def parent(p, c):
        e = e_ref[p]
        er = pltpu.roll(e, 64, 1)
        e0 = jnp.where(left, e, er); e1 = jnp.where(left, er, e)
        t0 = lax.dot_general(gd[2*p][:, :64], e0, NN, precision=HI, preferred_element_type=F32)
        t1 = lax.dot_general(gd[2*p+1][:, :64], e1, NN, precision=HI, preferred_element_type=F32)
        est = jnp.concatenate([e0,e1],0).T[:64]
        g = lax.dot_general(est, jnp.concatenate([t0,t1],0), NN, precision=HI, preferred_element_type=F32)
        nat[pl.ds((L+p)*32,32),:] = jnp.where(left32, g[:32], g[32:])
        return c
    lax.fori_loop(0, Pn, parent, 0, unroll=16)
    zeros = jnp.zeros((128-C,128), F32)
    for i in range(32):
        x = jnp.concatenate([nat[pl.ds(i, C, 32), :], zeros], 0).T
        a_ref[i] = x[:64]
        a_ref[i+32] = x[64:]
    live = lax.broadcasted_iota(jnp.int32, (1,128), 1) < C
    sub = lax.broadcasted_iota(jnp.int32, (8,128), 0)
    for p in range(8):
        b = 8*p
        T = [a_ref[b+kk, b:b+8, :] for kk in range(8)]
        for kk in range(8):
            inv = lax.rsqrt(jnp.where(live, T[kk][kk:kk+1,:], 1.0))
            row = jnp.where(sub >= kk, T[kk]*inv, 0.0)
            rinv_ref[pl.ds(b+kk,1), :] = inv
            r_ref[b+kk, b:b+8, :] = row
            for k2 in range(kk+1, 8):
                T[k2] = T[k2] - row[k2:k2+1,:]*row
        for q in range(p+1, 8):
            T = []
            for kk in range(8):
                s = a_ref[b+kk, 8*q:8*q+8, :]
                for t in range(kk):
                    s = s - r_ref[b+t, pl.ds(b+kk,1), :]*T[t]
                T.append(s*rinv_ref[pl.ds(b+kk,1), :])
                r_ref[b+kk, 8*q:8*q+8, :] = T[kk]
        r_out[p].start()
        for q in range(p+1, 8):
            def upd(h, c):
                i0 = 8*q + 4*h
                acc = [[a_ref[i0+u, 8*j:8*j+8, :] for j in range(q,8)] for u in range(4)]
                for kk in range(8):
                    v = [r_ref[b+kk, 8*j:8*j+8, :] for j in range(q,8)]
                    for u in range(4):
                        m = r_ref[b+kk, pl.ds(i0+u,1), :]
                        for j in range(8-q):
                            acc[u][j] = acc[u][j] - m*v[j]
                for u in range(4):
                    for j in range(q,8):
                        a_ref[i0+u, 8*j:8*j+8, :] = acc[u][j-q]
                return c
            lax.fori_loop(0, 2, upd, 0, unroll=True)
    row = lax.broadcasted_iota(jnp.int32, (C,128), 0)
    col = lax.broadcasted_iota(jnp.int32, (C,128), 1)
    eye = (row == col).astype(F32).astype(BF16)
    eye2 = jnp.concatenate([eye, eye], 1)
    for e in range(18):
        ch = jnp.concatenate([r_ref[k, 8*j:8*j+8, :] for k, j in chunk_tiles(e)], 0)
        hi, lo = split(ch)
        table_ref[e] = lax.dot_general(eye2, jnp.concatenate([hi,lo],1), NT, preferred_element_type=F32)
    for copy in r_out:
        copy.wait()

def factor(u, e):
    L, Pn = u.shape[0], e.shape[0]; C = L+Pn
    hbm = pl.BlockSpec(memory_space=pl.ANY)
    vmem = pl.BlockSpec(memory_space=pltpu.VMEM)
    dma = pltpu.SemaphoreType.DMA
    return pl.pallas_call(factor_kernel,
        in_specs=[hbm, hbm], out_specs=(vmem, hbm, vmem),
        out_shape=(jax.ShapeDtypeStruct((18,C,128),F32), jax.ShapeDtypeStruct((64,64,128),F32), jax.ShapeDtypeStruct((64,128),F32)),
        scratch_shapes=[pltpu.VMEM((C*32,128),F32), pltpu.VMEM((L,64,128),F32), pltpu.VMEM((64,64,128),F32),
                        pltpu.VMEM(u.shape,F32), pltpu.VMEM(e.shape,F32), pltpu.VMEM((64,64,128),F32), dma((4,)), dma, dma((8,))],
        **params(11, 60),
        name="factor")(u, e)

def unpack(v):
    lane = lax.broadcasted_iota(jnp.int32, (8,128), 1)
    sub = lax.broadcasted_iota(jnp.int32, (8,128), 0)
    half = lane & 63
    left = lane < 64
    v0, v1 = v[0:8], v[8:16]
    w0, w1 = pltpu.roll(v0, 64, 1), pltpu.roll(v1, 64, 1)
    y = jnp.where(sub < 4, v[16:17], v[17:18])
    z = pltpu.roll(pltpu.roll(y, 0, 1, stride=16, stride_axis=0), 0, 1, stride=16, stride_axis=0)
    parts = [
        jnp.where(left, v0, w0),
        jnp.where(left, v1, w1),
        jnp.where(left, w0, v0),
        jnp.where(left, w1, v1),
        jnp.where(left, z, pltpu.roll(z, 64, 1)),
        jnp.where(left, pltpu.roll(v1, 104, 1), pltpu.roll(v1, 40, 1)),
        jnp.where(left, pltpu.roll(v0, 112, 1), pltpu.roll(v0, 48, 1)),
        jnp.where(left, pltpu.roll(v1, 56, 1), pltpu.roll(v1, 120, 1)),
    ]
    return jnp.concatenate([x if p == 0 else jnp.where(half >= 8*p, x, 0.0) for p, x in enumerate(parts)], 0)

def mix(x):
    left = lax.broadcasted_iota(jnp.int32, x.shape, 1) < 64
    hi = x.astype(BF16).astype(F32)
    return jnp.where(left, hi, x - hi).astype(BF16)

def left_kernel(leaves, lrows_ref, prows_ref, tab_hbm, ls_hbm, ps_hbm, lout_hbm, pout_hbm,
                tab_ref, s_ref, p_ref, m_ref, lhs_ref, tsem, ssem, psem):
    total = lhs_ref.shape[0]
    chunks = s_ref.shape[0]//2
    tab_in = pltpu.make_async_copy(tab_hbm, tab_ref, tsem)
    def s_in(g):
        src, i = (ls_hbm, g) if g < chunks else (ps_hbm, g - chunks)
        return pltpu.make_async_copy(src.at[:, :, pl.ds(i*128, 128)], s_ref.at[g], ssem.at[g])
    def p_out(g):
        dst, i = (lout_hbm, g) if g < chunks else (pout_hbm, g - chunks)
        return pltpu.make_async_copy(p_ref.at[g], dst.at[pl.ds(i*128, 128)], psem.at[g])
    tab_in.start()
    for g in range(2*chunks):
        s_in(g).start()
    tab_in.wait()
    def prep(c, _):
        lhs_ref[c] = mix(unpack(tab_ref[pl.ds(c, 18, total), :]))
        return _
    lax.fori_loop(0, total, prep, 0, unroll=16)
    left = lax.broadcasted_iota(jnp.int32, (32,128), 1) < 64
    def chunk(g, carry):
        for i in range(2*chunks):
            @pl.when(g == i)
            def _():
                s_in(i).wait()
        for k in range(32):
            m_ref[pl.ds(k, 128, 40), :] = jnp.concatenate([s_ref[g, k], s_ref[g, k+32]], 0).T
        low = g < chunks
        start = jnp.where(low, g, g - chunks)*128
        def one(b, _):
            m = m_ref[pl.ds(pl.multiple_of(b*40, 8), 32), :]
            t = pltpu.roll(m, 64, 1)
            hi, lo = split(jnp.concatenate([jnp.where(left, m, t), jnp.where(left, t, m)], 0))
            a = lhs_ref[jnp.where(low, lrows_ref[start + b], leaves + prows_ref[start + b])]
            res = lax.dot_general(jnp.concatenate([a, a], 1), jnp.concatenate([hi,hi,lo,lo], 0), NN, preferred_element_type=F32)
            p_ref[g, b] = mix(res)
            return _
        lax.fori_loop(0, 128, one, 0, unroll=64)
        for i in range(2*chunks):
            @pl.when(g == i)
            def _():
                p_out(i).start()
        return carry
    lax.fori_loop(0, 2*chunks, chunk, 0)
    for g in range(2*chunks):
        p_out(g).wait()

def left_products(lrows, prows, table, lblocks, pblocks, leaves):
    total = table.shape[0]//18
    B = lblocks.shape[2]
    smem = pl.BlockSpec(memory_space=pltpu.SMEM)
    hbm = pl.BlockSpec(memory_space=pl.ANY)
    dma = pltpu.SemaphoreType.DMA
    n = 2*B//128
    return pl.pallas_call(functools.partial(left_kernel, leaves),
        in_specs=[smem, smem, hbm, hbm, hbm], out_specs=(hbm, hbm),
        out_shape=(jax.ShapeDtypeStruct((B,64,128), BF16),)*2,
        scratch_shapes=[pltpu.VMEM(table.shape,F32), pltpu.VMEM((n,64,64,128),F32), pltpu.VMEM((n,128,64,128),BF16),
                        pltpu.VMEM((128*40,128),F32), pltpu.VMEM((total,64,128),BF16), dma, dma((n,)), dma((n,))],
        **params(15, 60), name="left")(lrows, prows, table, lblocks, pblocks)

def close_kernel(caps, hi_ref, lslots_ref, pslots_ref, count_ref, near_hbm, far_hbm, lp_hbm, pp_hbm, lout_hbm, pout_hbm,
                 near_ref, far_ref, p_ref, out_ref, c_ref, w_ref, fsem, psem, osem):
    chunks = p_ref.shape[0]//2
    wide = sum(caps)
    peers = near_ref.shape[0]//(18*wide)
    offset = 2*peers*caps[0]
    near_in = pltpu.make_async_copy(near_hbm, near_ref, fsem.at[0])
    far_in = pltpu.make_async_copy(far_hbm, far_ref, fsem.at[1])
    def p_in(g):
        src, i = (lp_hbm, g) if g < chunks else (pp_hbm, g - chunks)
        return pltpu.make_async_copy(src.at[pl.ds(i*128, 128)], p_ref.at[g], psem.at[g])
    def out(g):
        dst, i = (lout_hbm, g) if g < chunks else (pout_hbm, g - chunks)
        return pltpu.make_async_copy(out_ref.at[g], dst.at[:, :, pl.ds(i*128, 128)], osem.at[g])
    near_in.start()
    far_in.start()
    for g in range(2*chunks):
        p_in(g).start()
    for side, copy, f_ref in ((0, near_in, near_ref), (1, far_in, far_ref)):
        copy.wait()
        first = jnp.where(hi_ref[0] == side, 0, peers)
        def prep(n, _):
            for t in range(wide):
                hi, lo = split(unpack(f_ref[pl.ds(n*18*wide + t, 18, wide), :]))
                spot = (first + n)*caps[0] + t if t < caps[0] else offset + (first + n)*caps[1] + t - caps[0]
                w_ref[spot] = jnp.concatenate([hi, lo], 1)
            return _
        lax.fori_loop(0, peers, prep, 0, unroll=max(1, 16//wide))
    lane = lax.broadcasted_iota(jnp.int32, (64,128), 1)
    def chunk(g, carry):
        for i in range(2*chunks):
            @pl.when(g == i)
            def _():
                p_in(i).wait()
        low = g < chunks
        start = jnp.where(low, g, g - chunks)*128
        def one(b, _):
            a = p_ref[g, b]
            w = w_ref[jnp.where(low, lslots_ref[start + b], offset + pslots_ref[start + b])]
            res = lax.dot_general(jnp.concatenate([a, a], 1), w, NT, preferred_element_type=F32)
            c_ref[pl.ds(pl.multiple_of(b*40, 8), 32), :] = jnp.concatenate([res[:32], res[32:]], 1)
            return _
        lax.fori_loop(0, 128, one, 0, unroll=64)
        live = lane + start < jnp.where(low, count_ref[0, 0], count_ref[0, 1])
        for i in range(32):
            x = c_ref[pl.ds(i, 128, 40), :].T
            out_ref[g, i] = jnp.where(live, x[:64], 0.0)
            out_ref[g, i+32] = jnp.where(live, x[64:], 0.0)
        for i in range(2*chunks):
            @pl.when(g == i)
            def _():
                out(i).start()
        return carry
    lax.fori_loop(0, 2*chunks, chunk, 0)
    for g in range(2*chunks):
        out(g).wait()

def close(hi, lslots, pslots, counts, near, far, lprods, pprods, caps):
    B = lprods.shape[0]
    n = 2*B//128
    total = 2*near.shape[0]//18
    smem = pl.BlockSpec(memory_space=pltpu.SMEM)
    hbm = pl.BlockSpec(memory_space=pl.ANY)
    dma = pltpu.SemaphoreType.DMA
    return pl.pallas_call(functools.partial(close_kernel, caps),
        in_specs=[smem]*4 + [hbm]*4, out_specs=(hbm, hbm),
        out_shape=(jax.ShapeDtypeStruct((64,64,B), F32),)*2,
        scratch_shapes=[pltpu.VMEM(near.shape,F32), pltpu.VMEM(far.shape,F32), pltpu.VMEM((n,128,64,128),BF16),
                        pltpu.VMEM((n,64,64,128),F32), pltpu.VMEM((128*40,128),F32), pltpu.VMEM((total,64,256),BF16),
                        dma((2,)), dma((n,)), dma((n,))],
        **params(19, 60), name="close")(hi, lslots, pslots, counts, near, far, lprods, pprods)

def gather_kernel(picks, lane_ref, idx_ref, table_ref, out_ref):
    peers, wide = idx_ref.shape[0], len(picks)
    C, lanes = table_ref.shape[1], idx_ref.shape[1]
    shape = (peers, wide, lanes)
    pick = lax.broadcasted_iota(jnp.int32, (1, wide, lanes), 1)
    want = jnp.zeros((1, wide, lanes), jnp.int32)
    base = jnp.zeros((1, wide, lanes), jnp.int32)
    for i, (which, t, b) in enumerate(picks):
        want = jnp.where(pick == i, lane_ref[which] + t, want)
        base = jnp.where(pick == i, b, base)
    lane = lax.broadcasted_iota(jnp.int32, shape, 2)
    idx = jnp.where(lane == want, idx_ref[...].reshape(peers, 1, lanes) + base, 0).astype(F32)
    idx = jnp.sum(idx, axis=2, keepdims=True).reshape(peers*wide, 1)
    col = lax.broadcasted_iota(jnp.int32, (peers*wide,128), 1).astype(F32)
    hot = (col == idx).astype(F32).astype(BF16)
    hot = jnp.concatenate([hot, hot], 1)
    pad = jnp.zeros((128-C, 128), F32)
    for e in range(18):
        hi, lo = split(jnp.concatenate([table_ref[e], pad], 0))
        res = lax.dot_general(hot, jnp.concatenate([hi, lo], 0), NN, preferred_element_type=F32)
        for q in range(peers):
            out_ref[pl.ds((q*18 + e)*wide, wide), :] = res[q*wide:(q+1)*wide]

def gather(lanes, idx, table, picks):
    peers, wide = idx.shape[0], len(picks)
    smem = pl.BlockSpec(memory_space=pltpu.SMEM)
    vmem = pl.BlockSpec(memory_space=pltpu.VMEM)
    return pl.pallas_call(functools.partial(gather_kernel, picks),
        in_specs=[smem, vmem, vmem], out_specs=vmem,
        out_shape=jax.ShapeDtypeStruct((peers*18*wide,128),F32),
        **params(2, 60), name="gather")(lanes, idx, table)

def basis_kernel(u_ref, e_ref, table_ref, r_ref, rinv_ref, basis_ref, nt_ref, x_ref, nat):
    L = u_ref.shape[0]; Pn = e_ref.shape[0]; C = L+Pn
    sub = lax.broadcasted_iota(jnp.int32, (8,128), 0)
    zero = jnp.zeros((8,128), F32)
    for q in range(8):
        def rows(h, _):
            acc = [[zero]*q for u in range(4)]
            for t in range(8*q):
                v = [x_ref[t, 8*j:8*j+8, :] for j in range(t//8+1)]
                for u in range(4):
                    m = r_ref[t, pl.ds(8*q+4*h+u,1), :]
                    for j in range(t//8+1):
                        acc[u][j] = acc[u][j] - m*v[j]
            for u in range(4):
                for j in range(q):
                    x_ref[8*q+4*h+u, 8*j:8*j+8, :] = acc[u][j]
            return _
        if q:
            lax.fori_loop(0, 2, rows, 0, unroll=True)
        for j in range(q+1):
            T = []
            for u in range(8):
                s = (sub == u).astype(F32) if j == q else x_ref[8*q+u, 8*j:8*j+8, :]
                for t in range(u):
                    s = s - r_ref[8*q+t, pl.ds(8*q+u,1), :]*T[t]
                T.append(s*rinv_ref[pl.ds(8*q+u,1), :])
                x_ref[8*q+u, 8*j:8*j+8, :] = T[u]
        for j in range(q+1, 8):
            for u in range(8):
                x_ref[8*q+u, 8*j:8*j+8, :] = zero
    for i in range(32):
        nat[pl.ds(i, C, 32), :] = jnp.concatenate([x_ref[i], x_ref[i+32]], 0).T[:C]
    left32 = lax.broadcasted_iota(jnp.int32, (32,128), 1) < 64
    left = lax.broadcasted_iota(jnp.int32, (64,128), 1) < 64
    def twice(m, first, wide):
        t = pltpu.roll(m, 64, 1)
        return jnp.where(wide, m, t) if first else jnp.where(wide, t, m)
    def inverse(c):
        m = nat[pl.ds(c*32,32),:]
        x = mix(jnp.concatenate([twice(m, True, left32), twice(m, False, left32)], 0))
        return jnp.concatenate([x, x], 1)
    def stack(x):
        hi, lo = split(x)
        return jnp.concatenate([hi,hi,lo,lo], 0)
    def leaf(l, _):
        basis_ref[l] = lax.dot_general(inverse(l), stack(u_ref[l]), NN, preferred_element_type=F32)
        return _
    lax.fori_loop(0, L, leaf, 0, unroll=32)
    def parent(p, _):
        e = e_ref[p]
        est = jnp.concatenate([twice(e, True, left), twice(e, False, left)],0).T[:64]
        w = lax.dot_general(inverse(L+p), stack(est), NN, preferred_element_type=F32)
        out = []
        for c in range(2):
            hi, lo = split(twice(w, c == 0, left))
            x = mix(unpack(table_ref[pl.ds(2*p+c, 18, C), :]))
            out.append(lax.dot_general(jnp.concatenate([x,x],1), jnp.concatenate([hi,lo],1), NT, preferred_element_type=F32))
        nt_ref[p] = jnp.concatenate(out, 1)
        return _
    lax.fori_loop(0, Pn, parent, 0, unroll=16)

def bases(u, e, table, r, rinv):
    C = u.shape[0]+e.shape[0]
    return pl.pallas_call(basis_kernel,
        out_shape=(jax.ShapeDtypeStruct(u.shape,F32), jax.ShapeDtypeStruct(e.shape,F32)),
        scratch_shapes=[pltpu.VMEM((64,64,128),F32), pltpu.VMEM((C*32,128),F32)],
        **params(9, 60), name="basis")(u, e, table, r, rinv)

def per_device(
    leaf_bases, transfers, leaf_blocks, parent_blocks, leaf_rows, leaf_slots, leaf_requests,
    parent_rows, parent_slots, parent_requests, block_counts,
):
    leaves = leaf_bases.shape[0]
    parents = transfers.shape[0]
    half = lax.axis_size("lo")
    slots, pslots = leaf_requests.shape[1], parent_requests.shape[1]
    cap, pcap = slots // (2 * half), pslots // (2 * half)
    hi = lax.axis_index("hi").astype(jnp.int32)
    here = hi * half + lax.axis_index("lo").astype(jnp.int32)
    there = (1 - hi) * half + lax.axis_index("lo").astype(jnp.int32)
    lanes = jnp.stack([here * cap, slots + here * pcap, there * cap, slots + there * pcap])
    wanted = jnp.broadcast_to(
        jnp.concatenate([leaf_requests, parent_requests], 1), (half, slots + pslots)
    )
    wanted = lax.all_to_all(wanted, "lo", 0, 0, tiled=True)
    table, r, rinv = factor(leaf_bases, transfers)
    swap = [(0, 1), (1, 0)]
    far_table = lax.ppermute(table, "hi", swap)
    picks = [(0, t, 0) for t in range(cap)] + [(1, t, leaves) for t in range(pcap)]
    near = gather(lanes, wanted, table, picks)
    near = lax.all_to_all(near, "lo", 0, 0, tiled=True)
    flat = table.reshape(-1, 128)
    leaf_left, parent_left = left_products(leaf_rows, parent_rows, flat, leaf_blocks, parent_blocks, leaves)
    far_table, parent_left, leaf_left = lax.optimization_barrier((far_table, parent_left, leaf_left))
    far = gather(lanes, wanted, far_table, [(which + 2, t, base) for which, t, base in picks])
    far = lax.all_to_all(far, "lo", 0, 0, tiled=True)
    leaf_basis, new_transfers = bases(leaf_bases, transfers, flat, r, rinv)
    leaf_coupling, parent_coupling = close(
        hi.reshape(1), leaf_slots, parent_slots, block_counts, near, far, leaf_left, parent_left, (cap, pcap)
    )
    return (leaf_basis, new_transfers, leaf_coupling, parent_coupling)


def solution(mesh):
    halves = jax.sharding.Mesh(mesh.devices.reshape(2, -1), ("hi", "lo"))
    leaf = ("hi", "lo")
    rows = P(leaf, None, None)
    blocks = P(None, None, leaf)
    ids = P(leaf)
    per_owner = P(leaf, None)
    return jax.shard_map(
        per_device,
        mesh=halves,
        in_specs=(rows, rows, blocks, blocks, ids, ids, per_owner, ids, ids, per_owner, per_owner),
        out_specs=(rows, rows, blocks, blocks),
        check_vma=False,
    )
```

```python
import functools

import jax
import jax.numpy as jnp
from jax import lax
from jax.experimental import pallas as pl
from jax.experimental.pallas import tpu as pltpu
from jax.sharding import PartitionSpec as P

F32=jnp.float32; BF16=jnp.bfloat16
HI=lax.Precision.HIGHEST
NT=(((1,),(1,)),((),()))
NN=(((1,),(0,)),((),()))

def seg_tiles(k, tiles):
    p, s = divmod(k, 8)
    low = [(8*(tiles-p)+s, jv) for jv in range(tiles-p, tiles)] if p else []
    return low + [(k, jv) for jv in range(p, tiles)]

def chunk_tiles(e):
    if e < 16:
        return seg_tiles(e, 8) + seg_tiles(e+16, 8)
    return [(32 + 4*(e-16) + s, jv) for s in (1, 0, 3, 2) for jv in range(4, 8)]

def params(us, mib):
    return dict(
        cost_estimate=pl.CostEstimate(flops=int(us*1.15e9), bytes_accessed=0, transcendentals=0),
        compiler_params=pltpu.CompilerParams(vmem_limit_bytes=mib*2**20),
    )

def split(x):
    hi = x.astype(BF16)
    return hi, (x - hi.astype(F32)).astype(BF16)

def factor_kernel(u_hbm, e_hbm, table_ref, r_hbm, rinv_ref, nat, gd, a_ref, u_ref, e_ref, r_ref, usem, esem, rsem):
    L = u_ref.shape[0]; Pn = e_ref.shape[0]; C = L+Pn
    part = L//4
    u_in = [pltpu.make_async_copy(u_hbm.at[pl.ds(i*part, part)], u_ref.at[pl.ds(i*part, part)], usem.at[i]) for i in range(4)]
    e_in = pltpu.make_async_copy(e_hbm, e_ref, esem)
    r_out = [pltpu.make_async_copy(r_ref.at[pl.ds(8*p, 8)], r_hbm.at[pl.ds(8*p, 8)], rsem.at[p]) for p in range(8)]
    for copy in u_in + [e_in]:
        copy.start()
    lane = lax.broadcasted_iota(jnp.int32, (64,128), 1)
    left = lane < 64
    left32 = left[:32]
    def gram(l, c):
        u = u_ref[l]
        g = lax.dot_general(u, jnp.concatenate([u,u],0), NT, precision=HI, preferred_element_type=F32)
        gd[l] = g
        nat[pl.ds(l*40,32),:] = jnp.where(left32, g[:32], g[32:])
        return c
    for i in range(4):
        u_in[i].wait()
        lax.fori_loop(i*part, (i+1)*part, gram, 0, unroll=part)
    e_in.wait()
    def parent(p, c):
        e = e_ref[p]
        er = pltpu.roll(e, 64, 1)
        e0 = jnp.where(left, e, er); e1 = jnp.where(left, er, e)
        t0 = lax.dot_general(gd[2*p][:, :64], e0, NN, precision=HI, preferred_element_type=F32)
        t1 = lax.dot_general(gd[2*p+1][:, :64], e1, NN, precision=HI, preferred_element_type=F32)
        est = jnp.concatenate([e0,e1],0).T[:64]
        g = lax.dot_general(est, jnp.concatenate([t0,t1],0), NN, precision=HI, preferred_element_type=F32)
        nat[pl.ds((L+p)*40,32),:] = jnp.where(left32, g[:32], g[32:])
        return c
    lax.fori_loop(0, Pn, parent, 0, unroll=16)
    zeros = jnp.zeros((128-C,128), F32)
    for i in range(32):
        x = jnp.concatenate([nat[pl.ds(i, C, 40), :], zeros], 0).T
        a_ref[i] = x[:64]
        a_ref[i+32] = x[64:]
    live = lax.broadcasted_iota(jnp.int32, (1,128), 1) < C
    sub = lax.broadcasted_iota(jnp.int32, (8,128), 0)
    for p in range(8):
        b = 8*p
        T = [a_ref[b+kk, b:b+8, :] for kk in range(8)]
        for kk in range(8):
            inv = lax.rsqrt(jnp.where(live, T[kk][kk:kk+1,:], 1.0))
            row = jnp.where(sub >= kk, T[kk]*inv, 0.0)
            rinv_ref[pl.ds(b+kk,1), :] = inv
            r_ref[b+kk, b:b+8, :] = row
            for k2 in range(kk+1, 8):
                T[k2] = T[k2] - row[k2:k2+1,:]*row
        for q in range(p+1, 8):
            T = []
            for kk in range(8):
                s = a_ref[b+kk, 8*q:8*q+8, :]
                for t in range(kk):
                    s = s - r_ref[b+t, pl.ds(b+kk,1), :]*T[t]
                T.append(s*rinv_ref[pl.ds(b+kk,1), :])
                r_ref[b+kk, 8*q:8*q+8, :] = T[kk]
        r_out[p].start()
        for q in range(p+1, 8):
            def upd(h, c):
                i0 = 8*q + 4*h
                acc = [[a_ref[i0+u, 8*j:8*j+8, :] for j in range(q,8)] for u in range(4)]
                for kk in range(8):
                    v = [r_ref[b+kk, 8*j:8*j+8, :] for j in range(q,8)]
                    for u in range(4):
                        m = r_ref[b+kk, pl.ds(i0+u,1), :]
                        for j in range(8-q):
                            acc[u][j] = acc[u][j] - m*v[j]
                for u in range(4):
                    for j in range(q,8):
                        a_ref[i0+u, 8*j:8*j+8, :] = acc[u][j-q]
                return c
            lax.fori_loop(0, 2, upd, 0, unroll=True)
    row = lax.broadcasted_iota(jnp.int32, (C,128), 0)
    col = lax.broadcasted_iota(jnp.int32, (C,128), 1)
    eye = (row == col).astype(F32).astype(BF16)
    eye2 = jnp.concatenate([eye, eye], 1)
    for e in range(18):
        ch = jnp.concatenate([r_ref[k, 8*j:8*j+8, :] for k, j in chunk_tiles(e)], 0)
        hi, lo = split(ch)
        table_ref[e] = lax.dot_general(eye2, jnp.concatenate([hi,lo],1), NT, preferred_element_type=F32)
    for copy in r_out:
        copy.wait()

def factor(u, e):
    L, Pn = u.shape[0], e.shape[0]; C = L+Pn
    hbm = pl.BlockSpec(memory_space=pl.ANY)
    vmem = pl.BlockSpec(memory_space=pltpu.VMEM)
    dma = pltpu.SemaphoreType.DMA
    return pl.pallas_call(factor_kernel,
        in_specs=[hbm, hbm], out_specs=(vmem, hbm, vmem),
        out_shape=(jax.ShapeDtypeStruct((18,C,128),F32), jax.ShapeDtypeStruct((64,64,128),F32), jax.ShapeDtypeStruct((64,128),F32)),
        scratch_shapes=[pltpu.VMEM((C*40,128),F32), pltpu.VMEM((L,64,128),F32), pltpu.VMEM((64,64,128),F32),
                        pltpu.VMEM(u.shape,F32), pltpu.VMEM(e.shape,F32), pltpu.VMEM((64,64,128),F32), dma((4,)), dma, dma((8,))],
        **params(11, 60),
        name="factor")(u, e)

def unpack(v):
    lane = lax.broadcasted_iota(jnp.int32, (8,128), 1)
    sub = lax.broadcasted_iota(jnp.int32, (8,128), 0)
    half = lane & 63
    left = lane < 64
    v0, v1 = v[0:8], v[8:16]
    w0, w1 = pltpu.roll(v0, 64, 1), pltpu.roll(v1, 64, 1)
    y = jnp.where(sub < 4, v[16:17], v[17:18])
    z = pltpu.roll(pltpu.roll(y, 0, 1, stride=16, stride_axis=0), 0, 1, stride=16, stride_axis=0)
    parts = [
        jnp.where(left, v0, w0),
        jnp.where(left, v1, w1),
        jnp.where(left, w0, v0),
        jnp.where(left, w1, v1),
        jnp.where(left, z, pltpu.roll(z, 64, 1)),
        jnp.where(left, pltpu.roll(v1, 104, 1), pltpu.roll(v1, 40, 1)),
        jnp.where(left, pltpu.roll(v0, 112, 1), pltpu.roll(v0, 48, 1)),
        jnp.where(left, pltpu.roll(v1, 56, 1), pltpu.roll(v1, 120, 1)),
    ]
    return jnp.concatenate([x if p == 0 else jnp.where(half >= 8*p, x, 0.0) for p, x in enumerate(parts)], 0)

def mix(x):
    left = lax.broadcasted_iota(jnp.int32, x.shape, 1) < 64
    hi = x.astype(BF16).astype(F32)
    return jnp.where(left, hi, x - hi).astype(BF16)

LEFT_US = 40

def left_kernel(base, total, rows_ref, tab_ref, s_hbm, out_hbm, s_ref, p_ref, m_ref, lhs_ref, ssem, psem):
    chunks = s_ref.shape[0]
    s_in = [pltpu.make_async_copy(s_hbm.at[:, :, pl.ds(g*128, 128)], s_ref.at[g], ssem.at[g]) for g in range(chunks)]
    p_out = [pltpu.make_async_copy(p_ref.at[g], out_hbm.at[pl.ds(g*128, 128)], psem.at[g]) for g in range(chunks)]
    for copy in s_in:
        copy.start()
    def prep(c, _):
        lhs_ref[c] = mix(unpack(tab_ref[pl.ds(base + c, 18, total), :]))
        return _
    lax.fori_loop(0, lhs_ref.shape[0], prep, 0, unroll=16)
    left = lax.broadcasted_iota(jnp.int32, (32,128), 1) < 64
    for g in range(chunks):
        s_in[g].wait()
        for k in range(32):
            m_ref[pl.ds(k, 128, 40), :] = jnp.concatenate([s_ref[g, k], s_ref[g, k+32]], 0).T
        def one(b, _):
            m = m_ref[pl.ds(pl.multiple_of(b*40, 8), 32), :]
            t = pltpu.roll(m, 64, 1)
            hi, lo = split(jnp.concatenate([jnp.where(left, m, t), jnp.where(left, t, m)], 0))
            a = lhs_ref[rows_ref[g*128 + b]]
            res = lax.dot_general(jnp.concatenate([a, a], 1), jnp.concatenate([hi,hi,lo,lo], 0), NN, preferred_element_type=F32)
            p_ref[g, b] = mix(res)
            return _
        lax.fori_loop(0, 128, one, 0, unroll=64)
        p_out[g].start()
    for copy in p_out:
        copy.wait()

def left_products(rows, table, blocks, base, clusters):
    total = table.shape[0]//18
    B = blocks.shape[2]
    n = B//128
    hbm = pl.BlockSpec(memory_space=pl.ANY)
    dma = pltpu.SemaphoreType.DMA
    return pl.pallas_call(functools.partial(left_kernel, base, total),
        in_specs=[pl.BlockSpec(memory_space=pltpu.SMEM), pl.BlockSpec(memory_space=pltpu.VMEM), hbm], out_specs=hbm,
        out_shape=jax.ShapeDtypeStruct((B,64,128), BF16),
        scratch_shapes=[pltpu.VMEM((n,64,64,128),F32), pltpu.VMEM((n,128,64,128),BF16),
                        pltpu.VMEM((128*40,128),F32), pltpu.VMEM((clusters,64,128),BF16), dma((n,)), dma((n,))],
        **params(LEFT_US, 60), name="left")(rows, table, blocks)

def weights(f_ref, first, stride):
    hi, lo = split(unpack(f_ref[pl.ds(first, 18, stride), :]))
    return jnp.concatenate([hi, lo], 1)

def unpack_kernel(caps, near_ref, w_hbm, w_ref, sem):
    wide = sum(caps)
    peers = near_ref.shape[0]//(18*wide)
    def prep(n, _):
        for t in range(wide):
            spot = n*caps[0] + t if t < caps[0] else peers*caps[0] + n*caps[1] + t - caps[0]
            w_ref[spot] = weights(near_ref, n*18*wide + t, wide)
        return _
    lax.fori_loop(0, peers, prep, 0, unroll=max(1, 16//wide))
    copy = pltpu.make_async_copy(w_ref, w_hbm, sem)
    copy.start()
    copy.wait()

def unpack_near(near, caps):
    total = near.shape[0]//18
    return pl.pallas_call(functools.partial(unpack_kernel, caps),
        in_specs=[pl.BlockSpec(memory_space=pltpu.VMEM)], out_specs=pl.BlockSpec(memory_space=pl.ANY),
        out_shape=jax.ShapeDtypeStruct((total,64,256), BF16),
        scratch_shapes=[pltpu.VMEM((total,64,256), BF16), pltpu.SemaphoreType.DMA],
        **params(5, 60), name="unpack")(near)

def close_kernel(caps, lslots_ref, pslots_ref, count_ref, near_hbm, far_ref, lp_hbm, pp_hbm, lout_hbm, pout_hbm,
                 p_ref, out_ref, c_ref, w_ref, wsem, psem, osem):
    chunks = p_ref.shape[0]//2
    wide = sum(caps)
    peers = far_ref.shape[0]//(18*wide)
    offset = 2*peers*caps[0]
    hi = lax.axis_index("hi")
    sizes = (peers*caps[0], peers*caps[1])
    w_in = [pltpu.make_async_copy(near_hbm.at[pl.ds(i*sizes[0], sizes[i])], w_ref.at[pl.ds(i*offset + hi*sizes[i], sizes[i])], wsem.at[i])
            for i in range(2)]
    def p_in(g):
        src, i = (lp_hbm, g) if g < chunks else (pp_hbm, g - chunks)
        return pltpu.make_async_copy(src.at[pl.ds(i*128, 128)], p_ref.at[g], psem.at[g])
    def out(g):
        dst, i = (lout_hbm, g) if g < chunks else (pout_hbm, g - chunks)
        return pltpu.make_async_copy(out_ref.at[g], dst.at[:, :, pl.ds(i*128, 128)], osem.at[g])
    for g in range(chunks):
        p_in(g).start()
    for copy in w_in:
        copy.start()
    for g in range(chunks, 2*chunks):
        p_in(g).start()
    def prep(n, _):
        device = (1 - hi)*peers + n
        for t in range(wide):
            spot = device*caps[0] + t if t < caps[0] else offset + device*caps[1] + t - caps[0]
            w_ref[spot] = weights(far_ref, n*18*wide + t, wide)
        return _
    lax.fori_loop(0, peers, prep, 0, unroll=max(1, 16//wide))
    for copy in w_in:
        copy.wait()
    lane = lax.broadcasted_iota(jnp.int32, (64,128), 1)
    def chunk(g, carry):
        for i in range(2*chunks):
            @pl.when(g == i)
            def _():
                p_in(i).wait()
        low = g < chunks
        start = jnp.where(low, g, g - chunks)*128
        def one(b, _):
            a = p_ref[g, b]
            w = w_ref[jnp.where(low, lslots_ref[start + b], offset + pslots_ref[start + b])]
            res = lax.dot_general(jnp.concatenate([a, a], 1), w, NT, preferred_element_type=F32)
            c_ref[pl.ds(pl.multiple_of(b*40, 8), 32), :] = jnp.concatenate([res[:32], res[32:]], 1)
            return _
        lax.fori_loop(0, 128, one, 0, unroll=64)
        live = lane + start < jnp.where(low, count_ref[0, 0], count_ref[0, 1])
        for i in range(32):
            x = c_ref[pl.ds(i, 128, 40), :].T
            out_ref[g, i] = jnp.where(live, x[:64], 0.0)
            out_ref[g, i+32] = jnp.where(live, x[64:], 0.0)
        for i in range(2*chunks):
            @pl.when(g == i)
            def _():
                out(i).start()
        return carry
    lax.fori_loop(0, 2*chunks, chunk, 0)
    for g in range(2*chunks):
        out(g).wait()

def close(lslots, pslots, counts, near, far, lprods, pprods, caps):
    B = lprods.shape[0]
    n = 2*B//128
    total = 2*near.shape[0]
    smem = pl.BlockSpec(memory_space=pltpu.SMEM)
    hbm = pl.BlockSpec(memory_space=pl.ANY)
    dma = pltpu.SemaphoreType.DMA
    return pl.pallas_call(functools.partial(close_kernel, caps),
        in_specs=[smem]*3 + [hbm, pl.BlockSpec(memory_space=pltpu.VMEM)] + [hbm]*2, out_specs=(hbm, hbm),
        out_shape=(jax.ShapeDtypeStruct((64,64,B), F32),)*2,
        scratch_shapes=[pltpu.VMEM((n,128,64,128),BF16),
                        pltpu.VMEM((n,64,64,128),F32), pltpu.VMEM((128*40,128),F32), pltpu.VMEM((total,64,256),BF16),
                        dma((2,)), dma((n,)), dma((n,))],
        **params(19, 60), name="close")(lslots, pslots, counts, near, far, lprods, pprods)

def gather_kernel(picks, sizes, far, idx_ref, table_ref, out_ref):
    peers, wide = idx_ref.shape[0], len(picks)
    C, lanes = table_ref.shape[1], idx_ref.shape[1]
    shape = (peers, wide, lanes)
    half, slots, cap, pcap = sizes
    hi = lax.axis_index("hi")
    side = 1 - hi if far else hi
    place = side*half + lax.axis_index("lo")
    starts = (place*cap, slots + place*pcap)
    pick = lax.broadcasted_iota(jnp.int32, (1, wide, lanes), 1)
    want = jnp.zeros((1, wide, lanes), jnp.int32)
    base = jnp.zeros((1, wide, lanes), jnp.int32)
    for i, (which, t, b) in enumerate(picks):
        want = jnp.where(pick == i, starts[which] + t, want)
        base = jnp.where(pick == i, b, base)
    lane = lax.broadcasted_iota(jnp.int32, shape, 2)
    idx = jnp.where(lane == want, idx_ref[...].reshape(peers, 1, lanes) + base, 0).astype(F32)
    idx = jnp.sum(idx, axis=2, keepdims=True).reshape(peers*wide, 1)
    col = lax.broadcasted_iota(jnp.int32, (peers*wide,128), 1).astype(F32)
    hot = (col == idx).astype(F32).astype(BF16)
    hot = jnp.concatenate([hot, hot], 1)
    pad = jnp.zeros((128-C, 128), F32)
    for e in range(18):
        hi, lo = split(jnp.concatenate([table_ref[e], pad], 0))
        res = lax.dot_general(hot, jnp.concatenate([hi, lo], 0), NN, preferred_element_type=F32)
        for q in range(peers):
            out_ref[pl.ds((q*18 + e)*wide, wide), :] = res[q*wide:(q+1)*wide]

def gather(idx, table, picks, sizes, far):
    peers, wide = idx.shape[0], len(picks)
    vmem = pl.BlockSpec(memory_space=pltpu.VMEM)
    return pl.pallas_call(functools.partial(gather_kernel, picks, sizes, far),
        in_specs=[vmem, vmem], out_specs=vmem,
        out_shape=jax.ShapeDtypeStruct((peers*18*wide,128),F32),
        **params(0.1, 60), name="gather")(idx, table)

def basis_kernel(u_hbm, e_hbm, table_ref, r_hbm, rinv_ref, basis_hbm, nt_hbm, x_ref, nat, u_ref, e_ref, r_ref, basis_ref, nt_ref, rsem, sem):
    L = u_ref.shape[0]; Pn = e_ref.shape[0]; C = L+Pn
    r_in = [pltpu.make_async_copy(r_hbm.at[pl.ds(8*p, 8)], r_ref.at[pl.ds(8*p, 8)], rsem.at[p]) for p in range(8)]
    u_in = pltpu.make_async_copy(u_hbm, u_ref, sem.at[0])
    e_in = pltpu.make_async_copy(e_hbm, e_ref, sem.at[1])
    basis_out = pltpu.make_async_copy(basis_ref, basis_hbm, sem.at[2])
    nt_out = pltpu.make_async_copy(nt_ref, nt_hbm, sem.at[3])
    for copy in r_in + [u_in, e_in]:
        copy.start()
    sub = lax.broadcasted_iota(jnp.int32, (8,128), 0)
    zero = jnp.zeros((8,128), F32)
    for q in range(8):
        r_in[q].wait()
        def rows(h, _):
            acc = [[zero]*q for u in range(4)]
            for t in range(8*q):
                v = [x_ref[t, 8*j:8*j+8, :] for j in range(t//8+1)]
                for u in range(4):
                    m = r_ref[t, pl.ds(8*q+4*h+u,1), :]
                    for j in range(t//8+1):
                        acc[u][j] = acc[u][j] - m*v[j]
            for u in range(4):
                for j in range(q):
                    x_ref[8*q+4*h+u, 8*j:8*j+8, :] = acc[u][j]
            return _
        if q:
            lax.fori_loop(0, 2, rows, 0, unroll=True)
        for j in range(q+1):
            T = []
            for u in range(8):
                s = (sub == u).astype(F32) if j == q else x_ref[8*q+u, 8*j:8*j+8, :]
                for t in range(u):
                    s = s - r_ref[8*q+t, pl.ds(8*q+u,1), :]*T[t]
                T.append(s*rinv_ref[pl.ds(8*q+u,1), :])
                x_ref[8*q+u, 8*j:8*j+8, :] = T[u]
        for j in range(q+1, 8):
            for u in range(8):
                x_ref[8*q+u, 8*j:8*j+8, :] = zero
    for i in range(32):
        nat[pl.ds(i, C, 40), :] = jnp.concatenate([x_ref[i], x_ref[i+32]], 0).T[:C]
    left32 = lax.broadcasted_iota(jnp.int32, (32,128), 1) < 64
    left = lax.broadcasted_iota(jnp.int32, (64,128), 1) < 64
    def twice(m, first, wide):
        t = pltpu.roll(m, 64, 1)
        return jnp.where(wide, m, t) if first else jnp.where(wide, t, m)
    def inverse(c):
        m = nat[pl.ds(c*40,32),:]
        x = mix(jnp.concatenate([twice(m, True, left32), twice(m, False, left32)], 0))
        return jnp.concatenate([x, x], 1)
    def stack(x):
        hi, lo = split(x)
        return jnp.concatenate([hi,hi,lo,lo], 0)
    def leaf(l, _):
        basis_ref[l] = lax.dot_general(inverse(l), stack(u_ref[l]), NN, preferred_element_type=F32)
        return _
    u_in.wait()
    lax.fori_loop(0, L, leaf, 0, unroll=32)
    basis_out.start()
    e_in.wait()
    def parent(p, _):
        e = e_ref[p]
        est = jnp.concatenate([twice(e, True, left), twice(e, False, left)],0).T[:64]
        w = lax.dot_general(inverse(L+p), stack(est), NN, preferred_element_type=F32)
        out = []
        for c in range(2):
            hi, lo = split(twice(w, c == 0, left))
            x = mix(unpack(table_ref[pl.ds(2*p+c, 18, C), :]))
            out.append(lax.dot_general(jnp.concatenate([x,x],1), jnp.concatenate([hi,lo],1), NT, preferred_element_type=F32))
        nt_ref[p] = jnp.concatenate(out, 1)
        return _
    lax.fori_loop(0, Pn, parent, 0, unroll=16)
    nt_out.start()
    basis_out.wait()
    nt_out.wait()

def bases(u, e, table, r, rinv):
    C = u.shape[0]+e.shape[0]
    hbm = pl.BlockSpec(memory_space=pl.ANY)
    vmem = pl.BlockSpec(memory_space=pltpu.VMEM)
    dma = pltpu.SemaphoreType.DMA
    return pl.pallas_call(basis_kernel,
        in_specs=[hbm, hbm, vmem, hbm, vmem], out_specs=(hbm, hbm),
        out_shape=(jax.ShapeDtypeStruct(u.shape,F32), jax.ShapeDtypeStruct(e.shape,F32)),
        scratch_shapes=[pltpu.VMEM((64,64,128),F32), pltpu.VMEM((C*40,128),F32), pltpu.VMEM(u.shape,F32), pltpu.VMEM(e.shape,F32),
                        pltpu.VMEM((64,64,128),F32), pltpu.VMEM(u.shape,F32), pltpu.VMEM(e.shape,F32), dma((8,)), dma((4,))],
        **params(9, 60), name="basis")(u, e, table, r, rinv)

def per_device(
    leaf_bases, transfers, leaf_blocks, parent_blocks, leaf_rows, leaf_slots, leaf_requests,
    parent_rows, parent_slots, parent_requests, block_counts,
):
    leaves = leaf_bases.shape[0]
    parents = transfers.shape[0]
    half = lax.axis_size("lo")
    slots, pslots = leaf_requests.shape[1], parent_requests.shape[1]
    cap, pcap = slots // (2 * half), pslots // (2 * half)
    wanted = jnp.concatenate(
        [jnp.broadcast_to(x, (half, x.shape[1])) for x in (leaf_requests, parent_requests)], 1
    )
    wanted = lax.all_to_all(wanted, "lo", 0, 0, tiled=True)
    table, r, rinv = factor(leaf_bases, transfers)
    far_table = lax.ppermute(table, "hi", [(0, 1), (1, 0)])
    picks = [(0, t, 0) for t in range(cap)] + [(1, t, leaves) for t in range(pcap)]
    sizes = (half, slots, cap, pcap)
    near = gather(wanted, table, picks, sizes, False)
    flat = lax.optimization_barrier((table, near))[0].reshape(-1, 128)
    near = lax.all_to_all(near, "lo", 0, 0, tiled=True)
    leaf_left = left_products(leaf_rows, flat, leaf_blocks, 0, leaves)
    parent_left = left_products(parent_rows, flat, parent_blocks, leaves, parents)
    far_table = lax.optimization_barrier((far_table, leaf_left, parent_left))[0]
    far = gather(wanted, far_table, picks, sizes, True)
    r = lax.optimization_barrier((r, far))[0]
    near = unpack_near(lax.optimization_barrier((near, far))[0], (cap, pcap))
    far = lax.all_to_all(far, "lo", 0, 0, tiled=True)
    leaf_basis, new_transfers = bases(leaf_bases, transfers, flat, r, rinv)
    leaf_coupling, parent_coupling = close(
        leaf_slots, parent_slots, block_counts, near, far, leaf_left, parent_left, (cap, pcap)
    )
    return (leaf_basis, new_transfers, leaf_coupling, parent_coupling)


def solution(mesh):
    halves = jax.sharding.Mesh(mesh.devices.reshape(2, -1), ("hi", "lo"))
    leaf = ("hi", "lo")
    rows = P(leaf, None, None)
    blocks = P(None, None, leaf)
    ids = P(leaf)
    per_owner = P(leaf, None)
    return jax.shard_map(
        per_device,
        mesh=halves,
        in_specs=(rows, rows, blocks, blocks, ids, ids, per_owner, ids, ids, per_owner, per_owner),
        out_specs=(rows, rows, blocks, blocks),
        check_vma=False,
    )
```

```python
import functools

import jax
import jax.numpy as jnp
from jax import lax
from jax.experimental import pallas as pl
from jax.experimental.pallas import tpu as pltpu
from jax.sharding import PartitionSpec as P

F32=jnp.float32; BF16=jnp.bfloat16
HI=lax.Precision.HIGHEST
NT=(((1,),(1,)),((),()))
NN=(((1,),(0,)),((),()))

def seg_tiles(k, tiles):
    p, s = divmod(k, 8)
    low = [(8*(tiles-p)+s, jv) for jv in range(tiles-p, tiles)] if p else []
    return low + [(k, jv) for jv in range(p, tiles)]

def chunk_tiles(e):
    if e < 16:
        return seg_tiles(e, 8) + seg_tiles(e+16, 8)
    return [(32 + 4*(e-16) + s, jv) for s in (1, 0, 3, 2) for jv in range(4, 8)]

def params(us, mib):
    return dict(
        cost_estimate=pl.CostEstimate(flops=int(us*1.15e9), bytes_accessed=0, transcendentals=0),
        compiler_params=pltpu.CompilerParams(vmem_limit_bytes=mib*2**20),
    )

def split(x):
    hi = x.astype(BF16)
    return hi, (x - hi.astype(F32)).astype(BF16)

def split3(x):
    h = x.astype(BF16)
    r = x - h.astype(F32)
    m = r.astype(BF16)
    return h, m, (r - m.astype(F32)).astype(BF16)

def stack3(x):
    h, m, w = split3(x)
    return jnp.concatenate([h,h,m,m,w,h], 0)

def factor_kernel(u_hbm, e_hbm, table_ref, r_hbm, rinv_ref, nat, gd, a_ref, u_ref, e_ref, r_ref, usem, esem, rsem):
    L = u_ref.shape[0]; Pn = e_ref.shape[0]; C = L+Pn
    part = L//2
    u_in = [pltpu.make_async_copy(u_hbm.at[pl.ds(i*part, part)], u_ref.at[pl.ds(i*part, part)], usem.at[i]) for i in range(2)]
    e_in = pltpu.make_async_copy(e_hbm, e_ref, esem)
    r_out = [pltpu.make_async_copy(r_ref.at[pl.ds(8*p, 8)], r_hbm.at[pl.ds(8*p, 8)], rsem.at[p]) for p in range(8)]
    for copy in u_in + [e_in]:
        copy.start()
    lane = lax.broadcasted_iota(jnp.int32, (64,128), 1)
    left = lane < 64
    left32 = left[:32]
    def gram(l, c):
        u = u_ref[l]
        h, m, w = split3(u)
        rows = jnp.concatenate([h,h,m,m,w,h], 1)
        g = lax.dot_general(jnp.concatenate([h,m,h,m,h,w], 1), jnp.concatenate([rows,rows],0), NT, preferred_element_type=F32)
        gd[l] = g
        nat[pl.ds(l*40,32),:] = jnp.where(left32, g[:32], g[32:])
        return c
    for i in range(2):
        u_in[i].wait()
        lax.fori_loop(i*part, (i+1)*part, gram, 0, unroll=part)
    e_in.wait()
    def parent(p, c):
        e = e_ref[p]
        er = pltpu.roll(e, 64, 1)
        e0 = jnp.where(left, e, er); e1 = jnp.where(left, er, e)
        def times(g, x):
            h, m, w = (y.astype(F32) for y in split3(g))
            hm, hw = jnp.where(left, h, m).astype(BF16), jnp.where(left, h, w).astype(BF16)
            return lax.dot_general(jnp.concatenate([hm,hm,hw], 1), stack3(x), NN, preferred_element_type=F32)
        t0 = times(gd[2*p], e0)
        t1 = times(gd[2*p+1], e1)
        est = jnp.concatenate([e0,e1],0).T[:64]
        h, m, w = split3(est)
        g = lax.dot_general(jnp.concatenate([h,m,h,m,h,w], 1), stack3(jnp.concatenate([t0,t1],0)), NN, preferred_element_type=F32)
        nat[pl.ds((L+p)*40,32),:] = jnp.where(left32, g[:32], g[32:])
        return c
    lax.fori_loop(0, Pn, parent, 0, unroll=16)
    zeros = jnp.zeros((128-C,128), F32)
    for i in range(32):
        x = jnp.concatenate([nat[pl.ds(i, C, 40), :], zeros], 0).T
        a_ref[i] = x[:64]
        a_ref[i+32] = x[64:]
    live = lax.broadcasted_iota(jnp.int32, (1,128), 1) < C
    sub = lax.broadcasted_iota(jnp.int32, (8,128), 0)
    for p in range(8):
        b = 8*p
        T = [a_ref[b+kk, b:b+8, :] for kk in range(8)]
        for kk in range(8):
            inv = lax.rsqrt(jnp.where(live, T[kk][kk:kk+1,:], 1.0))
            row = jnp.where(sub >= kk, T[kk]*inv, 0.0)
            rinv_ref[pl.ds(b+kk,1), :] = inv
            r_ref[b+kk, b:b+8, :] = row
            for k2 in range(kk+1, 8):
                T[k2] = T[k2] - row[k2:k2+1,:]*row
        for q in range(p+1, 8):
            T = []
            for kk in range(8):
                s = a_ref[b+kk, 8*q:8*q+8, :]
                for t in range(kk):
                    s = s - r_ref[b+t, pl.ds(b+kk,1), :]*T[t]
                T.append(s*rinv_ref[pl.ds(b+kk,1), :])
                r_ref[b+kk, 8*q:8*q+8, :] = T[kk]
        r_out[p].start()
        for q in range(p+1, 8):
            def upd(h, c):
                i0 = 8*q + 4*h
                acc = [[a_ref[i0+u, 8*j:8*j+8, :] for j in range(q,8)] for u in range(4)]
                for kk in range(8):
                    v = [r_ref[b+kk, 8*j:8*j+8, :] for j in range(q,8)]
                    for u in range(4):
                        m = r_ref[b+kk, pl.ds(i0+u,1), :]
                        for j in range(8-q):
                            acc[u][j] = acc[u][j] - m*v[j]
                for u in range(4):
                    for j in range(q,8):
                        a_ref[i0+u, 8*j:8*j+8, :] = acc[u][j-q]
                return c
            lax.fori_loop(0, 2, upd, 0, unroll=True)
    row = lax.broadcasted_iota(jnp.int32, (C,128), 0)
    col = lax.broadcasted_iota(jnp.int32, (C,128), 1)
    eye = (row == col).astype(F32).astype(BF16)
    eye2 = jnp.concatenate([eye, eye], 1)
    for e in range(18):
        ch = jnp.concatenate([r_ref[k, 8*j:8*j+8, :] for k, j in chunk_tiles(e)], 0)
        hi, lo = split(ch)
        table_ref[e] = lax.dot_general(eye2, jnp.concatenate([hi,lo],1), NT, preferred_element_type=F32)
    for copy in r_out:
        copy.wait()

def factor(u, e):
    L, Pn = u.shape[0], e.shape[0]; C = L+Pn
    hbm = pl.BlockSpec(memory_space=pl.ANY)
    vmem = pl.BlockSpec(memory_space=pltpu.VMEM)
    dma = pltpu.SemaphoreType.DMA
    return pl.pallas_call(factor_kernel,
        in_specs=[hbm, hbm], out_specs=(vmem, hbm, vmem),
        out_shape=(jax.ShapeDtypeStruct((18,C,128),F32), jax.ShapeDtypeStruct((64,64,128),F32), jax.ShapeDtypeStruct((64,128),F32)),
        scratch_shapes=[pltpu.VMEM((C*40,128),F32), pltpu.VMEM((L,64,128),F32), pltpu.VMEM((64,64,128),F32),
                        pltpu.VMEM(u.shape,F32), pltpu.VMEM(e.shape,F32), pltpu.VMEM((64,64,128),F32), dma((2,)), dma, dma((8,))],
        **params(11, 60),
        name="factor")(u, e)

def unpack(v):
    lane = lax.broadcasted_iota(jnp.int32, (8,128), 1)
    sub = lax.broadcasted_iota(jnp.int32, (8,128), 0)
    half = lane & 63
    left = lane < 64
    v0, v1 = v[0:8], v[8:16]
    w0, w1 = pltpu.roll(v0, 64, 1), pltpu.roll(v1, 64, 1)
    y = jnp.where(sub < 4, v[16:17], v[17:18])
    z = pltpu.roll(pltpu.roll(y, 0, 1, stride=16, stride_axis=0), 0, 1, stride=16, stride_axis=0)
    parts = [
        jnp.where(left, v0, w0),
        jnp.where(left, v1, w1),
        jnp.where(left, w0, v0),
        jnp.where(left, w1, v1),
        jnp.where(left, z, pltpu.roll(z, 64, 1)),
        jnp.where(left, pltpu.roll(v1, 104, 1), pltpu.roll(v1, 40, 1)),
        jnp.where(left, pltpu.roll(v0, 112, 1), pltpu.roll(v0, 48, 1)),
        jnp.where(left, pltpu.roll(v1, 56, 1), pltpu.roll(v1, 120, 1)),
    ]
    return jnp.concatenate([x if p == 0 else jnp.where(half >= 8*p, x, 0.0) for p, x in enumerate(parts)], 0)

def mix(x):
    left = lax.broadcasted_iota(jnp.int32, x.shape, 1) < 64
    hi = x.astype(BF16).astype(F32)
    return jnp.where(left, hi, x - hi).astype(BF16)

LEFT_US = 40

def left_kernel(base, total, rows_ref, tab_ref, s_hbm, out_hbm, s_ref, p_ref, m_ref, lhs_ref, ssem, psem):
    chunks = s_ref.shape[0]
    s_in = [pltpu.make_async_copy(s_hbm.at[:, :, pl.ds(g*128, 128)], s_ref.at[g], ssem.at[g]) for g in range(chunks)]
    p_out = [pltpu.make_async_copy(p_ref.at[g], out_hbm.at[pl.ds(g*128, 128)], psem.at[g]) for g in range(chunks)]
    for copy in s_in:
        copy.start()
    def prep(c, _):
        lhs_ref[c] = mix(unpack(tab_ref[pl.ds(base + c, 18, total), :]))
        return _
    lax.fori_loop(0, lhs_ref.shape[0], prep, 0, unroll=16)
    left = lax.broadcasted_iota(jnp.int32, (32,128), 1) < 64
    for g in range(chunks):
        s_in[g].wait()
        for k in range(32):
            m_ref[pl.ds(k, 128, 40), :] = jnp.concatenate([s_ref[g, k], s_ref[g, k+32]], 0).T
        def one(b, _):
            m = m_ref[pl.ds(pl.multiple_of(b*40, 8), 32), :]
            t = pltpu.roll(m, 64, 1)
            hi, lo = split(jnp.concatenate([jnp.where(left, m, t), jnp.where(left, t, m)], 0))
            a = lhs_ref[rows_ref[g*128 + b]]
            res = lax.dot_general(jnp.concatenate([a, a], 1), jnp.concatenate([hi,hi,lo,lo], 0), NN, preferred_element_type=F32)
            p_ref[g, b] = mix(res)
            return _
        lax.fori_loop(0, 128, one, 0, unroll=128)
        p_out[g].start()
    for copy in p_out:
        copy.wait()

def left_products(rows, table, blocks, base, clusters):
    total = table.shape[0]//18
    B = blocks.shape[2]
    n = B//128
    hbm = pl.BlockSpec(memory_space=pl.ANY)
    dma = pltpu.SemaphoreType.DMA
    return pl.pallas_call(functools.partial(left_kernel, base, total),
        in_specs=[pl.BlockSpec(memory_space=pltpu.SMEM), pl.BlockSpec(memory_space=pltpu.VMEM), hbm], out_specs=hbm,
        out_shape=jax.ShapeDtypeStruct((B,64,128), BF16),
        scratch_shapes=[pltpu.VMEM((n,64,64,128),F32), pltpu.VMEM((n,128,64,128),BF16),
                        pltpu.VMEM((128*40,128),F32), pltpu.VMEM((clusters,64,128),BF16), dma((n,)), dma((n,))],
        **params(LEFT_US, 60), name="left")(rows, table, blocks)

def weights(f_ref, first, stride):
    hi, lo = split(unpack(f_ref[pl.ds(first, 18, stride), :]))
    return jnp.concatenate([hi, lo], 1)

def unpack_kernel(caps, near_ref, w_hbm, w_ref, sem):
    wide = sum(caps)
    peers = near_ref.shape[0]//(18*wide)
    def prep(n, _):
        for t in range(wide):
            spot = n*caps[0] + t if t < caps[0] else peers*caps[0] + n*caps[1] + t - caps[0]
            w_ref[spot] = weights(near_ref, n*18*wide + t, wide)
        return _
    lax.fori_loop(0, peers, prep, 0, unroll=max(1, 16//wide))
    copy = pltpu.make_async_copy(w_ref, w_hbm, sem)
    copy.start()
    copy.wait()

def unpack_near(near, caps):
    total = near.shape[0]//18
    return pl.pallas_call(functools.partial(unpack_kernel, caps),
        in_specs=[pl.BlockSpec(memory_space=pltpu.VMEM)], out_specs=pl.BlockSpec(memory_space=pl.ANY),
        out_shape=jax.ShapeDtypeStruct((total,64,256), BF16),
        scratch_shapes=[pltpu.VMEM((total,64,256), BF16), pltpu.SemaphoreType.DMA],
        **params(5, 60), name="unpack")(near)

def close_kernel(caps, lslots_ref, pslots_ref, count_ref, near_hbm, far_ref, lp_hbm, pp_hbm, lout_hbm, pout_hbm,
                 p_ref, out_ref, c_ref, w_ref, wsem, psem, osem):
    chunks = p_ref.shape[0]//2
    wide = sum(caps)
    peers = far_ref.shape[0]//(18*wide)
    offset = 2*peers*caps[0]
    hi = lax.axis_index("hi")
    sizes = (peers*caps[0], peers*caps[1])
    w_in = [pltpu.make_async_copy(near_hbm.at[pl.ds(i*sizes[0], sizes[i])], w_ref.at[pl.ds(i*offset + hi*sizes[i], sizes[i])], wsem.at[i])
            for i in range(2)]
    def p_in(g):
        src, i = (lp_hbm, g) if g < chunks else (pp_hbm, g - chunks)
        return pltpu.make_async_copy(src.at[pl.ds(i*128, 128)], p_ref.at[g], psem.at[g])
    def out(g):
        dst, i = (lout_hbm, g) if g < chunks else (pout_hbm, g - chunks)
        return pltpu.make_async_copy(out_ref.at[g], dst.at[:, :, pl.ds(i*128, 128)], osem.at[g])
    for g in range(chunks):
        p_in(g).start()
    for copy in w_in:
        copy.start()
    for g in range(chunks, 2*chunks):
        p_in(g).start()
    def prep(n, _):
        device = (1 - hi)*peers + n
        for t in range(wide):
            spot = device*caps[0] + t if t < caps[0] else offset + device*caps[1] + t - caps[0]
            w_ref[spot] = weights(far_ref, n*18*wide + t, wide)
        return _
    lax.fori_loop(0, peers, prep, 0, unroll=max(1, 16//wide))
    for copy in w_in:
        copy.wait()
    lane = lax.broadcasted_iota(jnp.int32, (64,128), 1)
    def chunk(g, carry):
        for i in range(2*chunks):
            @pl.when(g == i)
            def _():
                p_in(i).wait()
        low = g < chunks
        start = jnp.where(low, g, g - chunks)*128
        def one(b, _):
            a = p_ref[g, b]
            w = w_ref[jnp.where(low, lslots_ref[start + b], offset + pslots_ref[start + b])]
            res = lax.dot_general(jnp.concatenate([a, a], 1), w, NT, preferred_element_type=F32)
            c_ref[pl.ds(pl.multiple_of(b*40, 8), 32), :] = jnp.concatenate([res[:32], res[32:]], 1)
            return _
        lax.fori_loop(0, 128, one, 0, unroll=128)
        live = lane + start < jnp.where(low, count_ref[0, 0], count_ref[0, 1])
        for i in range(32):
            x = c_ref[pl.ds(i, 128, 40), :].T
            out_ref[g, i] = jnp.where(live, x[:64], 0.0)
            out_ref[g, i+32] = jnp.where(live, x[64:], 0.0)
        for i in range(2*chunks):
            @pl.when(g == i)
            def _():
                out(i).start()
        return carry
    lax.fori_loop(0, 2*chunks, chunk, 0)
    for g in range(2*chunks):
        out(g).wait()

def close(lslots, pslots, counts, near, far, lprods, pprods, caps):
    B = lprods.shape[0]
    n = 2*B//128
    total = 2*near.shape[0]
    smem = pl.BlockSpec(memory_space=pltpu.SMEM)
    hbm = pl.BlockSpec(memory_space=pl.ANY)
    dma = pltpu.SemaphoreType.DMA
    return pl.pallas_call(functools.partial(close_kernel, caps),
        in_specs=[smem]*3 + [hbm, pl.BlockSpec(memory_space=pltpu.VMEM)] + [hbm]*2, out_specs=(hbm, hbm),
        out_shape=(jax.ShapeDtypeStruct((64,64,B), F32),)*2,
        scratch_shapes=[pltpu.VMEM((n,128,64,128),BF16),
                        pltpu.VMEM((n,64,64,128),F32), pltpu.VMEM((128*40,128),F32), pltpu.VMEM((total,64,256),BF16),
                        dma((2,)), dma((n,)), dma((n,))],
        **params(19, 51), name="close")(lslots, pslots, counts, near, far, lprods, pprods)

def gather_kernel(picks, sizes, far, idx_ref, table_ref, out_ref):
    peers, wide = idx_ref.shape[0], len(picks)
    C, lanes = table_ref.shape[1], idx_ref.shape[1]
    shape = (peers, wide, lanes)
    half, slots, cap, pcap = sizes
    hi = lax.axis_index("hi")
    side = 1 - hi if far else hi
    place = side*half + lax.axis_index("lo")
    starts = (place*cap, slots + place*pcap)
    pick = lax.broadcasted_iota(jnp.int32, (1, wide, lanes), 1)
    want = jnp.zeros((1, wide, lanes), jnp.int32)
    base = jnp.zeros((1, wide, lanes), jnp.int32)
    for i, (which, t, b) in enumerate(picks):
        want = jnp.where(pick == i, starts[which] + t, want)
        base = jnp.where(pick == i, b, base)
    lane = lax.broadcasted_iota(jnp.int32, shape, 2)
    idx = jnp.where(lane == want, idx_ref[...].reshape(peers, 1, lanes) + base, 0).astype(F32)
    idx = jnp.sum(idx, axis=2, keepdims=True).reshape(peers*wide, 1)
    col = lax.broadcasted_iota(jnp.int32, (peers*wide,128), 1).astype(F32)
    hot = (col == idx).astype(F32).astype(BF16)
    hot = jnp.concatenate([hot, hot], 1)
    pad = jnp.zeros((128-C, 128), F32)
    for e in range(18):
        hi, lo = split(jnp.concatenate([table_ref[e], pad], 0))
        res = lax.dot_general(hot, jnp.concatenate([hi, lo], 0), NN, preferred_element_type=F32)
        for q in range(peers):
            out_ref[pl.ds((q*18 + e)*wide, wide), :] = res[q*wide:(q+1)*wide]

def gather(idx, table, picks, sizes, far):
    peers, wide = idx.shape[0], len(picks)
    vmem = pl.BlockSpec(memory_space=pltpu.VMEM)
    return pl.pallas_call(functools.partial(gather_kernel, picks, sizes, far),
        in_specs=[vmem, vmem], out_specs=vmem,
        out_shape=jax.ShapeDtypeStruct((peers*18*wide,128),F32),
        **params(2, 16), name="gather")(idx, table)

def basis_kernel(u_hbm, e_hbm, table_ref, r_hbm, rinv_ref, basis_hbm, nt_hbm, x_ref, nat, u_ref, e_ref, r_ref, basis_ref, nt_ref, rsem, sem):
    L = u_ref.shape[0]; Pn = e_ref.shape[0]; C = L+Pn
    r_in = [pltpu.make_async_copy(r_hbm.at[pl.ds(8*p, 8)], r_ref.at[pl.ds(8*p, 8)], rsem.at[p]) for p in range(8)]
    u_in = pltpu.make_async_copy(u_hbm, u_ref, sem.at[0])
    e_in = pltpu.make_async_copy(e_hbm, e_ref, sem.at[1])
    basis_out = pltpu.make_async_copy(basis_ref, basis_hbm, sem.at[2])
    nt_out = pltpu.make_async_copy(nt_ref, nt_hbm, sem.at[3])
    for copy in r_in + [u_in, e_in]:
        copy.start()
    sub = lax.broadcasted_iota(jnp.int32, (8,128), 0)
    zero = jnp.zeros((8,128), F32)
    for q in range(8):
        r_in[q].wait()
        def rows(h, _):
            acc = [[zero]*q for u in range(4)]
            for t in range(8*q):
                v = [x_ref[t, 8*j:8*j+8, :] for j in range(t//8+1)]
                for u in range(4):
                    m = r_ref[t, pl.ds(8*q+4*h+u,1), :]
                    for j in range(t//8+1):
                        acc[u][j] = acc[u][j] - m*v[j]
            for u in range(4):
                for j in range(q):
                    x_ref[8*q+4*h+u, 8*j:8*j+8, :] = acc[u][j]
            return _
        if q:
            lax.fori_loop(0, 2, rows, 0, unroll=True)
        for j in range(q+1):
            T = []
            for u in range(8):
                s = (sub == u).astype(F32) if j == q else x_ref[8*q+u, 8*j:8*j+8, :]
                for t in range(u):
                    s = s - r_ref[8*q+t, pl.ds(8*q+u,1), :]*T[t]
                T.append(s*rinv_ref[pl.ds(8*q+u,1), :])
                x_ref[8*q+u, 8*j:8*j+8, :] = T[u]
        for j in range(q+1, 8):
            for u in range(8):
                x_ref[8*q+u, 8*j:8*j+8, :] = zero
    for i in range(32):
        nat[pl.ds(i, C, 40), :] = jnp.concatenate([x_ref[i], x_ref[i+32]], 0).T[:C]
    left32 = lax.broadcasted_iota(jnp.int32, (32,128), 1) < 64
    left = lax.broadcasted_iota(jnp.int32, (64,128), 1) < 64
    def twice(m, first, wide):
        t = pltpu.roll(m, 64, 1)
        return jnp.where(wide, m, t) if first else jnp.where(wide, t, m)
    def inverse(c):
        m = nat[pl.ds(c*40,32),:]
        x = mix(jnp.concatenate([twice(m, True, left32), twice(m, False, left32)], 0))
        return jnp.concatenate([x, x], 1)
    def stack(x):
        hi, lo = split(x)
        return jnp.concatenate([hi,hi,lo,lo], 0)
    def leaf(l, _):
        basis_ref[l] = lax.dot_general(inverse(l), stack(u_ref[l]), NN, preferred_element_type=F32)
        return _
    u_in.wait()
    lax.fori_loop(0, L, leaf, 0, unroll=32)
    basis_out.start()
    e_in.wait()
    def parent(p, _):
        e = e_ref[p]
        est = jnp.concatenate([twice(e, True, left), twice(e, False, left)],0).T[:64]
        w = lax.dot_general(inverse(L+p), stack(est), NN, preferred_element_type=F32)
        out = []
        for c in range(2):
            hi, lo = split(twice(w, c == 0, left))
            x = mix(unpack(table_ref[pl.ds(2*p+c, 18, C), :]))
            out.append(lax.dot_general(jnp.concatenate([x,x],1), jnp.concatenate([hi,lo],1), NT, preferred_element_type=F32))
        nt_ref[p] = jnp.concatenate(out, 1)
        return _
    lax.fori_loop(0, Pn, parent, 0, unroll=16)
    nt_out.start()
    basis_out.wait()
    nt_out.wait()

def bases(u, e, table, r, rinv):
    C = u.shape[0]+e.shape[0]
    hbm = pl.BlockSpec(memory_space=pl.ANY)
    vmem = pl.BlockSpec(memory_space=pltpu.VMEM)
    dma = pltpu.SemaphoreType.DMA
    return pl.pallas_call(basis_kernel,
        in_specs=[hbm, hbm, vmem, hbm, vmem], out_specs=(hbm, hbm),
        out_shape=(jax.ShapeDtypeStruct(u.shape,F32), jax.ShapeDtypeStruct(e.shape,F32)),
        scratch_shapes=[pltpu.VMEM((64,64,128),F32), pltpu.VMEM((C*40,128),F32), pltpu.VMEM(u.shape,F32), pltpu.VMEM(e.shape,F32),
                        pltpu.VMEM((64,64,128),F32), pltpu.VMEM(u.shape,F32), pltpu.VMEM(e.shape,F32), dma((8,)), dma((4,))],
        **params(9, 60), name="basis")(u, e, table, r, rinv)

def per_device(
    leaf_bases, transfers, leaf_blocks, parent_blocks, leaf_rows, leaf_slots, leaf_requests,
    parent_rows, parent_slots, parent_requests, block_counts,
):
    leaves = leaf_bases.shape[0]
    parents = transfers.shape[0]
    half = lax.axis_size("lo")
    slots, pslots = leaf_requests.shape[1], parent_requests.shape[1]
    cap, pcap = slots // (2 * half), pslots // (2 * half)
    wanted = jnp.concatenate(
        [jnp.broadcast_to(x, (half, x.shape[1])) for x in (leaf_requests, parent_requests)], 1
    )
    wanted = lax.all_to_all(wanted, "lo", 0, 0, tiled=True)
    table, r, rinv = factor(leaf_bases, transfers)
    far_table = lax.ppermute(table, "hi", [(0, 1), (1, 0)])
    picks = [(0, t, 0) for t in range(cap)] + [(1, t, leaves) for t in range(pcap)]
    sizes = (half, slots, cap, pcap)
    near = gather(wanted, table, picks, sizes, False)
    flat = lax.optimization_barrier((table, near))[0].reshape(-1, 128)
    near = lax.all_to_all(near, "lo", 0, 0, tiled=True)
    leaf_left = left_products(leaf_rows, flat, leaf_blocks, 0, leaves)
    parent_left = left_products(parent_rows, flat, parent_blocks, leaves, parents)
    far_table = lax.optimization_barrier((far_table, leaf_left, parent_left))[0]
    far = gather(wanted, far_table, picks, sizes, True)
    r = lax.optimization_barrier((r, far))[0]
    near = unpack_near(lax.optimization_barrier((near, far))[0], (cap, pcap))
    far = lax.all_to_all(far, "lo", 0, 0, tiled=True)
    leaf_basis, new_transfers = bases(leaf_bases, transfers, flat, r, rinv)
    leaf_coupling, parent_coupling = close(
        leaf_slots, parent_slots, block_counts, near, far, leaf_left, parent_left, (cap, pcap)
    )
    return (leaf_basis, new_transfers, leaf_coupling, parent_coupling)


def solution(mesh):
    halves = jax.sharding.Mesh(mesh.devices.reshape(2, -1), ("hi", "lo"))
    leaf = ("hi", "lo")
    rows = P(leaf, None, None)
    blocks = P(None, None, leaf)
    ids = P(leaf)
    per_owner = P(leaf, None)
    return jax.shard_map(
        per_device,
        mesh=halves,
        in_specs=(rows, rows, blocks, blocks, ids, ids, per_owner, ids, ids, per_owner, per_owner),
        out_specs=(rows, rows, blocks, blocks),
        check_vma=False,
    )
```

```python
import functools

import jax
import jax.numpy as jnp
from jax import lax
from jax.experimental import pallas as pl
from jax.experimental.pallas import tpu as pltpu
from jax.sharding import PartitionSpec as P

F32=jnp.float32; BF16=jnp.bfloat16
HI=lax.Precision.HIGHEST
NT=(((1,),(1,)),((),()))
NN=(((1,),(0,)),((),()))

def seg_tiles(k, tiles):
    p, s = divmod(k, 8)
    low = [(8*(tiles-p)+s, jv) for jv in range(tiles-p, tiles)] if p else []
    return low + [(k, jv) for jv in range(p, tiles)]

def chunk_tiles(e):
    if e < 16:
        return seg_tiles(e, 8) + seg_tiles(e+16, 8)
    return [(32 + 4*(e-16) + s, jv) for s in (1, 0, 3, 2) for jv in range(4, 8)]

def params(us, mib):
    return dict(
        cost_estimate=pl.CostEstimate(flops=int(us*1.15e9), bytes_accessed=0, transcendentals=0),
        compiler_params=pltpu.CompilerParams(vmem_limit_bytes=mib*2**20),
    )

def split(x):
    hi = x.astype(BF16)
    return hi, (x - hi.astype(F32)).astype(BF16)

def split3(x):
    h = x.astype(BF16)
    r = x - h.astype(F32)
    m = r.astype(BF16)
    return h, m, (r - m.astype(F32)).astype(BF16)

def stack3(x):
    h, m, w = split3(x)
    return jnp.concatenate([h,h,m,m,w,h], 0)

def factor_kernel(u_hbm, e_hbm, table_ref, r_hbm, rinv_ref, nat, gd, a_ref, u_ref, e_ref, r_ref, usem, esem, rsem):
    L = u_ref.shape[0]; Pn = e_ref.shape[0]; C = L+Pn
    part = L//2
    u_in = [pltpu.make_async_copy(u_hbm.at[pl.ds(i*part, part)], u_ref.at[pl.ds(i*part, part)], usem.at[i]) for i in range(2)]
    e_in = pltpu.make_async_copy(e_hbm, e_ref, esem)
    r_out = [pltpu.make_async_copy(r_ref.at[pl.ds(8*p, 8)], r_hbm.at[pl.ds(8*p, 8)], rsem.at[p]) for p in range(8)]
    for copy in u_in + [e_in]:
        copy.start()
    lane = lax.broadcasted_iota(jnp.int32, (64,128), 1)
    left = lane < 64
    left32 = left[:32]
    def gram(l, c):
        u = u_ref[l]
        h, m, w = split3(u)
        rows = jnp.concatenate([h,h,m,m,w,h], 1)
        g = lax.dot_general(jnp.concatenate([h,m,h,m,h,w], 1), jnp.concatenate([rows,rows],0), NT, preferred_element_type=F32)
        gd[l] = g
        nat[pl.ds(l*40,32),:] = jnp.where(left32, g[:32], g[32:])
        return c
    for i in range(2):
        u_in[i].wait()
        lax.fori_loop(i*part, (i+1)*part, gram, 0, unroll=part)
    e_in.wait()
    def parent(p, c):
        e = e_ref[p]
        er = pltpu.roll(e, 64, 1)
        e0 = jnp.where(left, e, er); e1 = jnp.where(left, er, e)
        def times(g, x):
            h, m, w = (y.astype(F32) for y in split3(g))
            hm, hw = jnp.where(left, h, m).astype(BF16), jnp.where(left, h, w).astype(BF16)
            return lax.dot_general(jnp.concatenate([hm,hm,hw], 1), stack3(x), NN, preferred_element_type=F32)
        t0 = times(gd[2*p], e0)
        t1 = times(gd[2*p+1], e1)
        est = jnp.concatenate([e0,e1],0).T[:64]
        h, m, w = split3(est)
        g = lax.dot_general(jnp.concatenate([h,m,h,m,h,w], 1), stack3(jnp.concatenate([t0,t1],0)), NN, preferred_element_type=F32)
        nat[pl.ds((L+p)*40,32),:] = jnp.where(left32, g[:32], g[32:])
        return c
    lax.fori_loop(0, Pn, parent, 0, unroll=16)
    zeros = jnp.zeros((128-C,128), F32)
    for i in range(32):
        x = jnp.concatenate([nat[pl.ds(i, C, 40), :], zeros], 0).T
        a_ref[i] = x[:64]
        a_ref[i+32] = x[64:]
    live = lax.broadcasted_iota(jnp.int32, (1,128), 1) < C
    sub = lax.broadcasted_iota(jnp.int32, (8,128), 0)
    for p in range(8):
        b = 8*p
        T = [a_ref[b+kk, b:b+8, :] for kk in range(8)]
        for kk in range(8):
            inv = lax.rsqrt(jnp.where(live, T[kk][kk:kk+1,:], 1.0))
            row = jnp.where(sub >= kk, T[kk]*inv, 0.0)
            rinv_ref[pl.ds(b+kk,1), :] = inv
            r_ref[b+kk, b:b+8, :] = row
            for k2 in range(kk+1, 8):
                T[k2] = T[k2] - row[k2:k2+1,:]*row
        for q in range(p+1, 8):
            T = []
            for kk in range(8):
                s = a_ref[b+kk, 8*q:8*q+8, :]
                for t in range(kk):
                    s = s - r_ref[b+t, pl.ds(b+kk,1), :]*T[t]
                T.append(s*rinv_ref[pl.ds(b+kk,1), :])
                r_ref[b+kk, 8*q:8*q+8, :] = T[kk]
        r_out[p].start()
        for q in range(p+1, 8):
            def upd(h, c):
                i0 = 8*q + 4*h
                acc = [[a_ref[i0+u, 8*j:8*j+8, :] for j in range(q,8)] for u in range(4)]
                for kk in range(8):
                    v = [r_ref[b+kk, 8*j:8*j+8, :] for j in range(q,8)]
                    for u in range(4):
                        m = r_ref[b+kk, pl.ds(i0+u,1), :]
                        for j in range(8-q):
                            acc[u][j] = acc[u][j] - m*v[j]
                for u in range(4):
                    for j in range(q,8):
                        a_ref[i0+u, 8*j:8*j+8, :] = acc[u][j-q]
                return c
            lax.fori_loop(0, 2, upd, 0, unroll=True)
    row = lax.broadcasted_iota(jnp.int32, (C,128), 0)
    col = lax.broadcasted_iota(jnp.int32, (C,128), 1)
    eye = (row == col).astype(F32).astype(BF16)
    eye2 = jnp.concatenate([eye, eye], 1)
    for e in range(18):
        ch = jnp.concatenate([r_ref[k, 8*j:8*j+8, :] for k, j in chunk_tiles(e)], 0)
        hi, lo = split(ch)
        table_ref[e] = lax.dot_general(eye2, jnp.concatenate([hi,lo],1), NT, preferred_element_type=F32)
    for copy in r_out:
        copy.wait()

def factor(u, e):
    L, Pn = u.shape[0], e.shape[0]; C = L+Pn
    hbm = pl.BlockSpec(memory_space=pl.ANY)
    vmem = pl.BlockSpec(memory_space=pltpu.VMEM)
    dma = pltpu.SemaphoreType.DMA
    return pl.pallas_call(factor_kernel,
        in_specs=[hbm, hbm], out_specs=(vmem, hbm, vmem),
        out_shape=(jax.ShapeDtypeStruct((18,C,128),F32), jax.ShapeDtypeStruct((64,64,128),F32), jax.ShapeDtypeStruct((64,128),F32)),
        scratch_shapes=[pltpu.VMEM((C*40,128),F32), pltpu.VMEM((L,64,128),F32), pltpu.VMEM((64,64,128),F32),
                        pltpu.VMEM(u.shape,F32), pltpu.VMEM(e.shape,F32), pltpu.VMEM((64,64,128),F32), dma((2,)), dma, dma((8,))],
        **params(11, 60),
        name="factor")(u, e)

def unpack(v):
    lane = lax.broadcasted_iota(jnp.int32, (8,128), 1)
    sub = lax.broadcasted_iota(jnp.int32, (8,128), 0)
    half = lane & 63
    left = lane < 64
    v0, v1 = v[0:8], v[8:16]
    w0, w1 = pltpu.roll(v0, 64, 1), pltpu.roll(v1, 64, 1)
    y = jnp.where(sub < 4, v[16:17], v[17:18])
    z = pltpu.roll(pltpu.roll(y, 0, 1, stride=16, stride_axis=0), 0, 1, stride=16, stride_axis=0)
    parts = [
        jnp.where(left, v0, w0),
        jnp.where(left, v1, w1),
        jnp.where(left, w0, v0),
        jnp.where(left, w1, v1),
        jnp.where(left, z, pltpu.roll(z, 64, 1)),
        jnp.where(left, pltpu.roll(v1, 104, 1), pltpu.roll(v1, 40, 1)),
        jnp.where(left, pltpu.roll(v0, 112, 1), pltpu.roll(v0, 48, 1)),
        jnp.where(left, pltpu.roll(v1, 56, 1), pltpu.roll(v1, 120, 1)),
    ]
    return jnp.concatenate([x if p == 0 else jnp.where(half >= 8*p, x, 0.0) for p, x in enumerate(parts)], 0)

def mix(x):
    left = lax.broadcasted_iota(jnp.int32, x.shape, 1) < 64
    hi = x.astype(BF16).astype(F32)
    return jnp.where(left, hi, x - hi).astype(BF16)

LEFT_US = 40

def left_kernel(base, total, rows_ref, tab_ref, s_hbm, out_hbm, s_ref, p_ref, m_ref, lhs_ref, ssem, psem):
    chunks = s_ref.shape[0]
    s_in = [pltpu.make_async_copy(s_hbm.at[:, :, pl.ds(g*128, 128)], s_ref.at[g], ssem.at[g]) for g in range(chunks)]
    p_out = [pltpu.make_async_copy(p_ref.at[g], out_hbm.at[pl.ds(g*128, 128)], psem.at[g]) for g in range(chunks)]
    for copy in s_in:
        copy.start()
    def prep(c, _):
        lhs_ref[c] = mix(unpack(tab_ref[pl.ds(base + c, 18, total), :]))
        return _
    lax.fori_loop(0, lhs_ref.shape[0], prep, 0, unroll=16)
    left = lax.broadcasted_iota(jnp.int32, (32,128), 1) < 64
    for g in range(chunks):
        s_in[g].wait()
        for k in range(32):
            m_ref[pl.ds(k, 128, 40), :] = jnp.concatenate([s_ref[g, k], s_ref[g, k+32]], 0).T
        def one(b, _):
            m = m_ref[pl.ds(pl.multiple_of(b*40, 8), 32), :]
            t = pltpu.roll(m, 64, 1)
            hi, lo = split(jnp.concatenate([jnp.where(left, m, t), jnp.where(left, t, m)], 0))
            a = lhs_ref[rows_ref[g*128 + b]]
            res = lax.dot_general(jnp.concatenate([a, a], 1), jnp.concatenate([hi,hi,lo,lo], 0), NN, preferred_element_type=F32)
            p_ref[g, b] = mix(res)
            return _
        lax.fori_loop(0, 128, one, 0, unroll=128)
        p_out[g].start()
    for copy in p_out:
        copy.wait()

def left_products(rows, table, blocks, base, clusters):
    total = table.shape[0]//18
    B = blocks.shape[2]
    n = B//128
    hbm = pl.BlockSpec(memory_space=pl.ANY)
    dma = pltpu.SemaphoreType.DMA
    return pl.pallas_call(functools.partial(left_kernel, base, total),
        in_specs=[pl.BlockSpec(memory_space=pltpu.SMEM), pl.BlockSpec(memory_space=pltpu.VMEM), hbm], out_specs=hbm,
        out_shape=jax.ShapeDtypeStruct((B,64,128), BF16),
        scratch_shapes=[pltpu.VMEM((n,64,64,128),F32), pltpu.VMEM((n,128,64,128),BF16),
                        pltpu.VMEM((128*40,128),F32), pltpu.VMEM((clusters,64,128),BF16), dma((n,)), dma((n,))],
        **params(LEFT_US, 60), name="left")(rows, table, blocks)

def weights(f_ref, first, stride):
    hi, lo = split(unpack(f_ref[pl.ds(first, 18, stride), :]))
    return jnp.concatenate([hi, lo], 1)

def unpack_kernel(caps, near_ref, w_hbm, w_ref, sem):
    wide = sum(caps)
    peers = near_ref.shape[0]//(18*wide)
    def prep(n, _):
        for t in range(wide):
            spot = n*caps[0] + t if t < caps[0] else peers*caps[0] + n*caps[1] + t - caps[0]
            w_ref[spot] = weights(near_ref, n*18*wide + t, wide)
        return _
    lax.fori_loop(0, peers, prep, 0, unroll=max(1, 16//wide))
    copy = pltpu.make_async_copy(w_ref, w_hbm, sem)
    copy.start()
    copy.wait()

def unpack_near(near, caps):
    total = near.shape[0]//18
    return pl.pallas_call(functools.partial(unpack_kernel, caps),
        in_specs=[pl.BlockSpec(memory_space=pltpu.VMEM)], out_specs=pl.BlockSpec(memory_space=pl.ANY),
        out_shape=jax.ShapeDtypeStruct((total,64,256), BF16),
        scratch_shapes=[pltpu.VMEM((total,64,256), BF16), pltpu.SemaphoreType.DMA],
        **params(5, 60), name="unpack")(near)

def close_kernel(caps, lslots_ref, pslots_ref, count_ref, near_hbm, far_ref, lp_hbm, pp_hbm, lout_hbm, pout_hbm,
                 p_ref, out_ref, c_ref, w_ref, wsem, psem, osem):
    chunks = p_ref.shape[0]//2
    wide = sum(caps)
    peers = far_ref.shape[0]//(18*wide)
    offset = 2*peers*caps[0]
    hi = lax.axis_index("hi")
    sizes = (peers*caps[0], peers*caps[1])
    w_in = [pltpu.make_async_copy(near_hbm.at[pl.ds(i*sizes[0], sizes[i])], w_ref.at[pl.ds(i*offset + hi*sizes[i], sizes[i])], wsem.at[i])
            for i in range(2)]
    def p_in(g):
        src, i = (lp_hbm, g) if g < chunks else (pp_hbm, g - chunks)
        return pltpu.make_async_copy(src.at[pl.ds(i*128, 128)], p_ref.at[g], psem.at[g])
    def out(g, part):
        dst, i = (lout_hbm, g) if g < chunks else (pout_hbm, g - chunks)
        rows = pl.ds(16*part, 16)
        return pltpu.make_async_copy(out_ref.at[g, rows], dst.at[rows, :, pl.ds(i*128, 128)], osem.at[g, part])
    for g in range(chunks):
        p_in(g).start()
    for copy in w_in:
        copy.start()
    for g in range(chunks, 2*chunks):
        p_in(g).start()
    def prep(n, _):
        device = (1 - hi)*peers + n
        for t in range(wide):
            spot = device*caps[0] + t if t < caps[0] else offset + device*caps[1] + t - caps[0]
            w_ref[spot] = weights(far_ref, n*18*wide + t, wide)
        return _
    lax.fori_loop(0, peers, prep, 0, unroll=max(1, 16//wide))
    for copy in w_in:
        copy.wait()
    lane = lax.broadcasted_iota(jnp.int32, (64,128), 1)
    def chunk(g, carry):
        for i in range(2*chunks):
            @pl.when(g == i)
            def _():
                p_in(i).wait()
        low = g < chunks
        start = jnp.where(low, g, g - chunks)*128
        def one(b, _):
            a = p_ref[g, b]
            w = w_ref[jnp.where(low, lslots_ref[start + b], offset + pslots_ref[start + b])]
            res = lax.dot_general(jnp.concatenate([a, a], 1), w, NT, preferred_element_type=F32)
            c_ref[pl.ds(pl.multiple_of(b*40, 8), 32), :] = jnp.concatenate([res[:32], res[32:]], 1)
            return _
        lax.fori_loop(0, 128, one, 0, unroll=128)
        live = lane + start < jnp.where(low, count_ref[0, 0], count_ref[0, 1])
        for half in range(2):
            for i in range(16*half, 16*half + 16):
                x = c_ref[pl.ds(i, 128, 40), :].T
                out_ref[g, i] = jnp.where(live, x[:64], 0.0)
                out_ref[g, i+32] = jnp.where(live, x[64:], 0.0)
            for i in range(2*chunks):
                @pl.when(g == i)
                def _():
                    out(i, half).start()
                    out(i, half + 2).start()
        return carry
    lax.fori_loop(0, 2*chunks, chunk, 0)
    for g in range(2*chunks):
        for part in range(4):
            out(g, part).wait()

def close(lslots, pslots, counts, near, far, lprods, pprods, caps):
    B = lprods.shape[0]
    n = 2*B//128
    total = 2*near.shape[0]
    smem = pl.BlockSpec(memory_space=pltpu.SMEM)
    hbm = pl.BlockSpec(memory_space=pl.ANY)
    dma = pltpu.SemaphoreType.DMA
    return pl.pallas_call(functools.partial(close_kernel, caps),
        in_specs=[smem]*3 + [hbm, pl.BlockSpec(memory_space=pltpu.VMEM)] + [hbm]*2, out_specs=(hbm, hbm),
        out_shape=(jax.ShapeDtypeStruct((64,64,B), F32),)*2,
        scratch_shapes=[pltpu.VMEM((n,128,64,128),BF16),
                        pltpu.VMEM((n,64,64,128),F32), pltpu.VMEM((128*40,128),F32), pltpu.VMEM((total,64,256),BF16),
                        dma((2,)), dma((n,)), dma((n,4))],
        **params(19, 51), name="close")(lslots, pslots, counts, near, far, lprods, pprods)

def gather_kernel(picks, sizes, far, idx_ref, table_ref, out_ref):
    peers, wide = idx_ref.shape[0], len(picks)
    C, lanes = table_ref.shape[1], idx_ref.shape[1]
    shape = (peers, wide, lanes)
    half, slots, cap, pcap = sizes
    hi = lax.axis_index("hi")
    side = 1 - hi if far else hi
    place = side*half + lax.axis_index("lo")
    starts = (place*cap, slots + place*pcap)
    pick = lax.broadcasted_iota(jnp.int32, (1, wide, lanes), 1)
    want = jnp.zeros((1, wide, lanes), jnp.int32)
    base = jnp.zeros((1, wide, lanes), jnp.int32)
    for i, (which, t, b) in enumerate(picks):
        want = jnp.where(pick == i, starts[which] + t, want)
        base = jnp.where(pick == i, b, base)
    lane = lax.broadcasted_iota(jnp.int32, shape, 2)
    idx = jnp.where(lane == want, idx_ref[...].reshape(peers, 1, lanes) + base, 0).astype(F32)
    idx = jnp.sum(idx, axis=2, keepdims=True).reshape(peers*wide, 1)
    col = lax.broadcasted_iota(jnp.int32, (peers*wide,128), 1).astype(F32)
    hot = (col == idx).astype(F32).astype(BF16)
    hot = jnp.concatenate([hot, hot], 1)
    pad = jnp.zeros((128-C, 128), F32)
    for e in range(18):
        hi, lo = split(jnp.concatenate([table_ref[e], pad], 0))
        res = lax.dot_general(hot, jnp.concatenate([hi, lo], 0), NN, preferred_element_type=F32)
        for q in range(peers):
            out_ref[pl.ds((q*18 + e)*wide, wide), :] = res[q*wide:(q+1)*wide]

def gather(idx, table, picks, sizes, far):
    peers, wide = idx.shape[0], len(picks)
    vmem = pl.BlockSpec(memory_space=pltpu.VMEM)
    return pl.pallas_call(functools.partial(gather_kernel, picks, sizes, far),
        in_specs=[vmem, vmem], out_specs=vmem,
        out_shape=jax.ShapeDtypeStruct((peers*18*wide,128),F32),
        **params(2, 16), name="gather")(idx, table)

def basis_kernel(u_hbm, e_hbm, table_ref, r_hbm, rinv_ref, basis_hbm, nt_hbm, x_ref, nat, u_ref, e_ref, r_ref, basis_ref, nt_ref, rsem, sem):
    L = u_ref.shape[0]; Pn = e_ref.shape[0]; C = L+Pn
    r_in = [pltpu.make_async_copy(r_hbm.at[pl.ds(8*p, 8)], r_ref.at[pl.ds(8*p, 8)], rsem.at[p]) for p in range(8)]
    u_in = pltpu.make_async_copy(u_hbm, u_ref, sem.at[0])
    e_in = pltpu.make_async_copy(e_hbm, e_ref, sem.at[1])
    basis_out = pltpu.make_async_copy(basis_ref, basis_hbm, sem.at[2])
    nt_out = pltpu.make_async_copy(nt_ref, nt_hbm, sem.at[3])
    for copy in r_in + [u_in, e_in]:
        copy.start()
    sub = lax.broadcasted_iota(jnp.int32, (8,128), 0)
    zero = jnp.zeros((8,128), F32)
    for q in range(8):
        r_in[q].wait()
        def rows(h, _):
            acc = [[zero]*q for u in range(4)]
            for t in range(8*q):
                v = [x_ref[t, 8*j:8*j+8, :] for j in range(t//8+1)]
                for u in range(4):
                    m = r_ref[t, pl.ds(8*q+4*h+u,1), :]
                    for j in range(t//8+1):
                        acc[u][j] = acc[u][j] - m*v[j]
            for u in range(4):
                for j in range(q):
                    x_ref[8*q+4*h+u, 8*j:8*j+8, :] = acc[u][j]
            return _
        if q:
            lax.fori_loop(0, 2, rows, 0, unroll=True)
        for j in range(q+1):
            T = []
            for u in range(8):
                s = (sub == u).astype(F32) if j == q else x_ref[8*q+u, 8*j:8*j+8, :]
                for t in range(u):
                    s = s - r_ref[8*q+t, pl.ds(8*q+u,1), :]*T[t]
                T.append(s*rinv_ref[pl.ds(8*q+u,1), :])
                x_ref[8*q+u, 8*j:8*j+8, :] = T[u]
        for j in range(q+1, 8):
            for u in range(8):
                x_ref[8*q+u, 8*j:8*j+8, :] = zero
    for i in range(32):
        nat[pl.ds(i, C, 40), :] = jnp.concatenate([x_ref[i], x_ref[i+32]], 0).T[:C]
    left32 = lax.broadcasted_iota(jnp.int32, (32,128), 1) < 64
    left = lax.broadcasted_iota(jnp.int32, (64,128), 1) < 64
    def twice(m, first, wide):
        t = pltpu.roll(m, 64, 1)
        return jnp.where(wide, m, t) if first else jnp.where(wide, t, m)
    def inverse(c):
        m = nat[pl.ds(c*40,32),:]
        x = mix(jnp.concatenate([twice(m, True, left32), twice(m, False, left32)], 0))
        return jnp.concatenate([x, x], 1)
    def stack(x):
        hi, lo = split(x)
        return jnp.concatenate([hi,hi,lo,lo], 0)
    def leaf(l, _):
        basis_ref[l] = lax.dot_general(inverse(l), stack(u_ref[l]), NN, preferred_element_type=F32)
        return _
    u_in.wait()
    lax.fori_loop(0, L, leaf, 0, unroll=32)
    basis_out.start()
    e_in.wait()
    def parent(p, _):
        e = e_ref[p]
        est = jnp.concatenate([twice(e, True, left), twice(e, False, left)],0).T[:64]
        w = lax.dot_general(inverse(L+p), stack(est), NN, preferred_element_type=F32)
        out = []
        for c in range(2):
            hi, lo = split(twice(w, c == 0, left))
            x = mix(unpack(table_ref[pl.ds(2*p+c, 18, C), :]))
            out.append(lax.dot_general(jnp.concatenate([x,x],1), jnp.concatenate([hi,lo],1), NT, preferred_element_type=F32))
        nt_ref[p] = jnp.concatenate(out, 1)
        return _
    lax.fori_loop(0, Pn, parent, 0, unroll=16)
    nt_out.start()
    basis_out.wait()
    nt_out.wait()

def bases(u, e, table, r, rinv):
    C = u.shape[0]+e.shape[0]
    hbm = pl.BlockSpec(memory_space=pl.ANY)
    vmem = pl.BlockSpec(memory_space=pltpu.VMEM)
    dma = pltpu.SemaphoreType.DMA
    return pl.pallas_call(basis_kernel,
        in_specs=[hbm, hbm, vmem, hbm, vmem], out_specs=(hbm, hbm),
        out_shape=(jax.ShapeDtypeStruct(u.shape,F32), jax.ShapeDtypeStruct(e.shape,F32)),
        scratch_shapes=[pltpu.VMEM((64,64,128),F32), pltpu.VMEM((C*40,128),F32), pltpu.VMEM(u.shape,F32), pltpu.VMEM(e.shape,F32),
                        pltpu.VMEM((64,64,128),F32), pltpu.VMEM(u.shape,F32), pltpu.VMEM(e.shape,F32), dma((8,)), dma((4,))],
        **params(9, 60), name="basis")(u, e, table, r, rinv)

def per_device(
    leaf_bases, transfers, leaf_blocks, parent_blocks, leaf_rows, leaf_slots, leaf_requests,
    parent_rows, parent_slots, parent_requests, block_counts,
):
    leaves = leaf_bases.shape[0]
    parents = transfers.shape[0]
    half = lax.axis_size("lo")
    slots, pslots = leaf_requests.shape[1], parent_requests.shape[1]
    cap, pcap = slots // (2 * half), pslots // (2 * half)
    wanted = jnp.concatenate(
        [jnp.broadcast_to(x, (half, x.shape[1])) for x in (leaf_requests, parent_requests)], 1
    )
    wanted = lax.all_to_all(wanted, "lo", 0, 0, tiled=True)
    table, r, rinv = factor(leaf_bases, transfers)
    far_table = lax.ppermute(table, "hi", [(0, 1), (1, 0)])
    picks = [(0, t, 0) for t in range(cap)] + [(1, t, leaves) for t in range(pcap)]
    sizes = (half, slots, cap, pcap)
    near = gather(wanted, table, picks, sizes, False)
    flat = lax.optimization_barrier((table, near))[0].reshape(-1, 128)
    near = lax.all_to_all(near, "lo", 0, 0, tiled=True)
    leaf_left = left_products(leaf_rows, flat, leaf_blocks, 0, leaves)
    parent_left = left_products(parent_rows, flat, parent_blocks, leaves, parents)
    far_table = lax.optimization_barrier((far_table, leaf_left, parent_left))[0]
    far = gather(wanted, far_table, picks, sizes, True)
    r = lax.optimization_barrier((r, far))[0]
    near = unpack_near(lax.optimization_barrier((near, far))[0], (cap, pcap))
    far = lax.all_to_all(far, "lo", 0, 0, tiled=True)
    leaf_basis, new_transfers = bases(leaf_bases, transfers, flat, r, rinv)
    leaf_coupling, parent_coupling = close(
        leaf_slots, parent_slots, block_counts, near, far, leaf_left, parent_left, (cap, pcap)
    )
    return (leaf_basis, new_transfers, leaf_coupling, parent_coupling)


def solution(mesh):
    halves = jax.sharding.Mesh(mesh.devices.reshape(2, -1), ("hi", "lo"))
    leaf = ("hi", "lo")
    rows = P(leaf, None, None)
    blocks = P(None, None, leaf)
    ids = P(leaf)
    per_owner = P(leaf, None)
    return jax.shard_map(
        per_device,
        mesh=halves,
        in_specs=(rows, rows, blocks, blocks, ids, ids, per_owner, ids, ids, per_owner, per_owner),
        out_specs=(rows, rows, blocks, blocks),
        check_vma=False,
    )
```
